256 devices in a mesh: rep: 16 (over z, x_hi), space: 16 (over y, x_lo, core).
Axes of the slice: x: 4 (x_hi: 2, x_lo: 2; x = x_hi * 2 + x_lo), y: 4, z: 8, core: 2. Of those that a mesh axis runs over, the one named last changes fastest.
Arguments:
- positions: float32 [16, 3, 32, 4, 4, 128], P('rep', None, 'space'), may hold values from 0 to 1
- velocities: float32 [16, 3, 32, 4, 4, 128], P('rep', None, 'space'), may hold values from -12 to 12
- thermal_noise: float32 [16, 1, 3, 32, 4, 4, 128], P('rep', None, None, 'space'), may hold values from -6 to 6
- counts: int32 [32, 4, 4], P('space'), may hold values from 64 to 128, as said below
- pair_flags: int32 [13, 32, 4, 4], P(None, 'space'), may hold values 0 or 1
- exit_replica: int32 [16], replicated, may hold values from 0 to 15, each once
Outputs:
- quench_pos: float32 [16, 3, 32, 4, 4, 128], P('rep', None, 'space')
- quench_vel: float32 [16, 3, 32, 4, 4, 128], P('rep', None, 'space')
- dephase_pos: float32 [16, 3, 32, 4, 4, 128], P('rep', None, 'space')
- dephase_vel: float32 [16, 3, 32, 4, 4, 128], P('rep', None, 'space')
The draws below stay inside these ranges and needn't reach their ends.
Inputs may be any that keep to these rules, and one draw needn't show every extreme that they name: `counts`: the cell with the lowest indices of every aligned slab of 2 planes along the first dimension holds 128 atoms. `exit_replica`: every replica appears exactly once.
All inputs are finite; a program needn't handle non-finite values. No bound on the sum of `pair_flags` on one device may be relied on, other than what follows from the above.
Results may differ from the reference program's by a relative error of at most 0.0003.
Values sent between devices are 32-bit elements; how exact they have to be, the bound alone decides.
A program may use at most 128 MiB of HBM per device.

```python
import math
import jax
import jax.numpy as jnp
from jax import lax

SLOTS = 128
CX_DEV = 2
GY = 4
GZ = 4
HALF = 13
QUENCH = 2
DEPHASE = 1
REPS = 16
NX = 32


def draw_velocities(key, part):
    base = jax.random.normal(key, (REPS, 3, NX, GY, GZ, SLOTS), jnp.float32)
    ramp = 1.0 + 2.0 * jnp.arange(NX, dtype=jnp.float32) / NX
    ramp_full = ramp[None, None, :, None, None, None]
    return jnp.clip(base * ramp_full, -12.0, 12.0)


def draw_counts(key, part):
    raw = jax.random.randint(key, (NX, GY, GZ), SLOTS // 2, SLOTS + 1)
    plane = lax_free_iota(NX, 0)
    row = lax_free_iota(GY, 1)
    col = lax_free_iota(GZ, 2)
    first = (plane % CX_DEV == 0) & (row == 0) & (col == 0)
    return jnp.where(first, SLOTS, raw).astype(jnp.int32)


def lax_free_iota(length, where):
    shape = [1, 1, 1]
    shape[where] = length
    return jnp.arange(length, dtype=jnp.int32).reshape(shape)


def plant(drawn, stream_key, low, high):
    shape = drawn.shape
    spot = [jax.random.randint(jax.random.fold_in(stream_key, axis), (), 0, shape[axis]) for axis in range(len(shape))]
    drawn = drawn.at[tuple(spot)].set(low)
    longest = shape.index(max(shape))
    spot[longest] = (spot[longest] + 1) % shape[longest]
    return drawn.at[tuple(spot)].set(high)


def block_levels(key, dims, shards, least, largest):
    def one(axis_at, blocks):
        steps = jax.random.uniform(jax.random.fold_in(jax.random.fold_in(key, 6), axis_at), (blocks,), jnp.float32, least / len(shards), largest / len(shards))
        return jnp.repeat(jnp.exp(steps), dims[axis_at] // blocks).reshape((-1,) + (1,) * (len(dims) - axis_at - 1))

    loudness = one(*shards[0])
    for cut in shards[1:]:
        loudness = loudness * one(*cut)
    return loudness


def centred(key, extent, scale, limit, cuts=(), kind=jnp.bfloat16):
    values = scale * jax.random.normal(key, extent, jnp.float32)
    if cuts:
        values = values * block_levels(key, extent, cuts, -0.22, 0.18)
    return jnp.clip(values, -limit, limit).astype(kind)


def setup_inputs(seed: int = 0) -> dict:
    arg_keys = jax.random.split(jax.random.key(seed), 7)
    positions = jnp.clip(1.0 * jax.random.uniform(arg_keys[0], (REPS, 3, NX, GY, GZ, SLOTS), jnp.float32) ** block_levels(arg_keys[0], (REPS, 3, NX, GY, GZ, SLOTS), ((0, 16), (2, 16)), -0.2, 0.2), 0.0, 1.0)
    velocities = draw_velocities(jax.random.fold_in(arg_keys[6], 71), 0)
    thermal_noise = centred(arg_keys[2], (REPS, DEPHASE, 3, NX, GY, GZ, SLOTS), 1.0, 6.0, ((0, 16), (3, 16)), jnp.float32)
    counts = draw_counts(jax.random.fold_in(arg_keys[6], 71), 0)
    pair_flags = plant((jax.random.randint(arg_keys[4], (HALF, NX, GY, GZ), 0, 4) < 3).astype(jnp.int32), jax.random.fold_in(arg_keys[4], 1), 0, 1)
    exit_replica = jax.random.permutation(arg_keys[5], REPS).astype(jnp.int32)
    return {"positions": positions, "velocities": velocities, "thermal_noise": thermal_noise, "counts": counts, "pair_flags": pair_flags, "exit_replica": exit_replica}


CUTOFF_SQ = 1.0
PAIR_A = 3.0
STEP_SIZE = 0.1
ALPHA_MIX = 0.25
EPSILON = 1e-06
FRICTION = math.exp(-0.2)
KICK_SCALE = math.sqrt(1.0 - FRICTION * FRICTION)
HALF_OFFSETS = [(1, p, q) for p in (-1, 0, 1) for q in (-1, 0, 1)] + [(0, 1, q) for q in (-1, 0, 1)] + [(0, 0, 1)]

def flag_lookup(ox, oy, oz):
    for index, entry in enumerate(HALF_OFFSETS):
        if entry == (ox, oy, oz):
            return (index, True)
        if entry == (-ox, -oy, -oz):
            return (index, False)
    return (0, True)

def plane_pass(pos_win, occ_win, flag_win, embed_win):
    slot_count = pos_win.shape[-1]
    center = pos_win[:, 1]
    occ_self = occ_win[1]
    diagonal = 1.0 - jnp.eye(slot_count, dtype=jnp.float32)
    if embed_win is None:
        result = jnp.zeros(occ_self.shape, jnp.float32)
    else:
        result = jnp.zeros(center.shape, jnp.float32)
        embed_self = embed_win[1]
    for ox in (-1, 0, 1):
        for oy in (-1, 0, 1):
            for oz in (-1, 0, 1):
                moved = (-oy, -oz)
                partner = jnp.roll(pos_win[:, 1 + ox], moved, axis=(1, 2))
                lattice = jnp.array([ox, oy, oz], dtype=jnp.float32)[:, None, None, None, None]
                displace = center[..., :, None] - partner[..., None, :] - lattice
                squared = lax.optimization_barrier(jnp.sum(displace * displace, axis=0))
                occ_peer = jnp.roll(occ_win[1 + ox], moved, axis=(0, 1))
                weight = occ_self[..., :, None] * occ_peer[..., None, :]
                if ox == 0 and oy == 0 and (oz == 0):
                    weight = weight * diagonal
                else:
                    index, forward = flag_lookup(ox, oy, oz)
                    if forward:
                        flag = flag_win[index, 1]
                    else:
                        flag = jnp.roll(flag_win[index, 1 + ox], moved, axis=(0, 1))
                    weight = weight * flag[..., None, None]
                closeness = jnp.maximum(1.0 - squared / CUTOFF_SQ, 0.0)
                if embed_win is None:
                    result = result + lax.optimization_barrier(jnp.sum(weight * closeness * closeness * closeness, axis=-1)) / slot_count
                else:
                    embed_peer = jnp.roll(embed_win[1 + ox], moved, axis=(0, 1))
                    slope = weight * (-4.0 * PAIR_A * closeness * closeness * closeness - 3.0 * (embed_self[..., :, None] + embed_peer[..., None, :]) * closeness * closeness) / slot_count
                    result = result - 2.0 * lax.optimization_barrier(jnp.sum(slope[None] * displace, axis=-1))
    return result

def blocked(pos_win, occ_win, flag_win, embed_win):
    planes = pos_win.shape[1] - 2

    def one_plane(index):
        part_pos = lax.dynamic_slice_in_dim(pos_win, index, 3, 1)
        part_occ = lax.dynamic_slice_in_dim(occ_win, index, 3, 0)
        part_flag = lax.dynamic_slice_in_dim(flag_win, index, 3, 1)
        part_embed = None if embed_win is None else lax.dynamic_slice_in_dim(embed_win, index, 3, 0)
        return plane_pass(part_pos, part_occ, part_flag, part_embed)
    stacked = lax.map(one_plane, jnp.arange(planes, dtype=jnp.int32))
    if embed_win is None:
        return stacked
    return jnp.moveaxis(stacked, 0, 1)

def periodic(array, width, axis_cells):
    total = array.shape[axis_cells]
    head = lax.slice_in_dim(array, total - width, total, axis=axis_cells)
    tail = lax.slice_in_dim(array, 0, width, axis=axis_cells)
    return jnp.concatenate([head, array, tail], axis=axis_cells)

def force_of(coords, occupied, flag_float):
    pos_pad = periodic(coords, 1, 1)
    occ_pad = periodic(occupied, 1, 0)
    flag_pad = periodic(flag_float, 1, 1)
    density = blocked(pos_pad, occ_pad, flag_pad, None)
    embed = -1.0 / jnp.sqrt(1.0 + density)
    return blocked(pos_pad, occ_pad, flag_pad, periodic(embed, 1, 0))

def reference(positions, velocities, thermal_noise, counts, pair_flags, exit_replica):
    slot_count = positions.shape[-1]
    occupied = (jnp.arange(slot_count, dtype=jnp.int32) < counts[..., None]).astype(jnp.float32)
    flag_float = pair_flags.astype(jnp.float32)

    def quench(pair):
        coords = pair[0]
        motion = pair[1] * occupied[None]
        for quench_step in range(QUENCH):
            forces = force_of(coords, occupied, flag_float)
            motion = motion + STEP_SIZE * forces
            mixing = jnp.sqrt(jnp.sum(motion * motion) / (jnp.sum(forces * forces) + EPSILON))
            motion = (1.0 - ALPHA_MIX) * motion + ALPHA_MIX * mixing * forces
            coords = coords + STEP_SIZE * motion
        return (coords, motion)
    quench_pos, quench_vel = lax.map(quench, (positions, velocities))
    chosen = exit_replica[0]
    exit_pos = lax.dynamic_index_in_dim(positions, chosen, 0, keepdims=False)
    exit_vel = lax.dynamic_index_in_dim(velocities, chosen, 0, keepdims=False) * occupied[None]
    exit_force = force_of(exit_pos, occupied, flag_float)

    def dephase(noise_rep):
        coords, motion, forces = (exit_pos, exit_vel, exit_force)
        for dephase_step in range(DEPHASE):
            if dephase_step > 0:
                forces = force_of(coords, occupied, flag_float)
            motion = motion + STEP_SIZE * forces
            motion = FRICTION * motion + KICK_SCALE * occupied[None] * noise_rep[dephase_step]
            coords = coords + STEP_SIZE * motion
        return (coords, motion)
    dephase_pos, dephase_vel = lax.map(dephase, thermal_noise)
    return (quench_pos, quench_vel, dephase_pos, dephase_vel)
```

```python
import math

import jax
import jax.numpy as jnp
from jax import lax
from jax.experimental import pallas as pl
from jax.experimental.pallas import tpu as pltpu
from jax.sharding import PartitionSpec as P

QUENCH = 2
STEP_SIZE = 0.1
ALPHA_MIX = 0.25
EPSILON = 1e-06
FRICTION = math.exp(-0.2)
KICK_SCALE = math.sqrt(1.0 - FRICTION * FRICTION)

HALF_OFFSETS = (
    [(1, p, q) for p in (-1, 0, 1) for q in (-1, 0, 1)]
    + [(0, 1, q) for q in (-1, 0, 1)]
    + [(0, 0, 1)]
)
OFFSETS = [(p, q, r) for p in (-1, 0, 1) for q in (-1, 0, 1) for r in (-1, 0, 1)]
FAR = -1.0e6
LEFT = (0, 1, 2, 0, 1, 0)
RIGHT = (0, 0, 0, 1, 1, 2)
DEPTH = 48
F32, BF16 = jnp.float32, jnp.bfloat16


def flag_lookup(o):
    if o in HALF_OFFSETS:
        return HALF_OFFSETS.index(o), True
    return HALF_OFFSETS.index((-o[0], -o[1], -o[2])), False


def pieces(v):
    p1 = v.astype(BF16).astype(F32)
    r = v - p1
    p2 = r.astype(BF16).astype(F32)
    return p1, p2, r - p2


def split_rows(v, order):
    p = pieces(v)
    return jnp.concatenate([p[i] for i in order], axis=0)


def prepare_partners(pos_ref, count_ref, embed_ref, left_ref, mom_ref):
    lane = lax.broadcasted_iota(jnp.int32, (1, 128), 1)
    ones = jnp.ones((1, 128), F32)
    zeros = jnp.zeros((1, 128), F32)

    def one(j, carry):
        x = pos_ref[0, pl.ds(j, 1), :]
        y = pos_ref[1, pl.ds(j, 1), :]
        z = pos_ref[2, pl.ds(j, 1), :]
        live = lane < count_ref[j]
        norm = jnp.where(live, -(x * x + y * y + z * z), FAR)
        x = jnp.where(live, x, 0.0)
        y = jnp.where(live, y, 0.0)
        z = jnp.where(live, z, 0.0)
        e = zeros if embed_ref is None else jnp.where(live, embed_ref[pl.ds(j, 1), :], 0.0)
        v = jnp.concatenate([x, y, z, norm, ones, e, zeros, zeros], axis=0)
        p = pieces(v)
        table = jnp.concatenate([p[i] for i in LEFT], axis=0)
        left_ref[j] = table.T.astype(BF16)
        if mom_ref is not None:
            mom_ref[j] = jnp.concatenate([p[0], p[1]], axis=0).astype(BF16)
        return carry

    lax.fori_loop(0, 64, one, 0)


def centre_rows(pos_ref, i):
    x = pos_ref[0, pl.ds(i, 1), :]
    y = pos_ref[1, pl.ds(i, 1), :]
    z = pos_ref[2, pl.ds(i, 1), :]
    return x, y, z


def neighbour(c, o):
    cp, cy, cz = c // 16, (c // 4) % 4, c % 4
    return (cp + 1 + o[0]) * 16 + ((cy + o[1]) % 4 if isinstance(c, int) else ((cy + o[1] + 4) & 3)) * 4 + ((cz + o[2] + 4) & 3)


def density_kernel(pos_ref, count_ref, flag_ref, embed_ref, left_ref):
    prepare_partners(pos_ref, count_ref, None, left_ref, None)
    ones = jnp.ones((1, 128), F32)
    zeros = jnp.zeros((3, 128), F32)

    def one(c, carry):
        i = c + 16
        x, y, z = centre_rows(pos_ref, i)
        total = jnp.zeros((8, 128), F32)
        for o in OFFSETS:
            j = neighbour(c, o)
            dx, dy, dz = x - o[0], y - o[1], z - o[2]
            own = 1.0 - (dx * dx + dy * dy + dz * dz)
            if o != (0, 0, 0):
                h, forward = flag_lookup(o)
                flag = flag_ref[h, i] if forward else flag_ref[h, j]
                own = jnp.where(flag > 0, own, FAR)
            w = jnp.concatenate([2.0 * dx, 2.0 * dy, 2.0 * dz, ones, own, zeros], axis=0)
            right = split_rows(w, RIGHT).astype(BF16)
            m = jnp.dot(left_ref[j], right, preferred_element_type=F32)
            t = jnp.maximum(m, 0.0)
            if o == (0, 0, 0):
                rows = lax.broadcasted_iota(jnp.int32, (128, 128), 0)
                cols = lax.broadcasted_iota(jnp.int32, (128, 128), 1)
                t = jnp.where(rows == cols, 0.0, t)
            total = total + jnp.sum((t * t * t).reshape(16, 8, 128), axis=0)
        density = jnp.sum(total, axis=0, keepdims=True) / 128.0
        embed_ref[pl.ds(c, 1), :] = -0.25 * lax.rsqrt(1.0 + density)
        return carry

    lax.fori_loop(0, 32, one, 0)


def force_kernel(pos_ref, count_ref, flag_ref, embed_ref, force_ref, left_ref, mom_ref):
    prepare_partners(pos_ref, count_ref, embed_ref, left_ref, mom_ref)
    ones = jnp.ones((1, 128), F32)
    zero = jnp.zeros((1, 128), F32)
    lane = lax.broadcasted_iota(jnp.int32, (1, 128), 1)

    def one(c, carry):
        i = c + 16
        x, y, z = centre_rows(pos_ref, i)
        e = embed_ref[pl.ds(i, 1), :]
        fx = zero
        fy = zero
        fz = zero
        for o in OFFSETS:
            j = neighbour(c, o)
            dx, dy, dz = x - o[0], y - o[1], z - o[2]
            own = 1.0 - (dx * dx + dy * dy + dz * dz)
            if o != (0, 0, 0):
                h, forward = flag_lookup(o)
                flag = flag_ref[h, i] if forward else flag_ref[h, j]
                own = jnp.where(flag > 0, own, FAR)
            w = jnp.concatenate([2.0 * dx, 2.0 * dy, 2.0 * dz, ones, own, zero, zero, zero], axis=0)
            u = jnp.concatenate([2.0 * dx, 2.0 * dy, 2.0 * dz, ones, own + e, ones, zero, zero], axis=0)
            right = jnp.concatenate([split_rows(w, RIGHT), split_rows(u, RIGHT)], axis=1).astype(BF16)
            both = jnp.dot(left_ref[j], right, preferred_element_type=F32)
            t = jnp.maximum(both[:, :128], 0.0)
            if o == (0, 0, 0):
                rows = lax.broadcasted_iota(jnp.int32, (128, 128), 0)
                cols = lax.broadcasted_iota(jnp.int32, (128, 128), 1)
                t = jnp.where(rows == cols, 0.0, t)
            g = t * t * both[:, 128:]
            hi = g.astype(BF16)
            lo = (g - hi.astype(F32)).astype(BF16)
            mom = mom_ref[j]
            s = jnp.dot(mom, hi, preferred_element_type=F32) + jnp.dot(mom, lo, preferred_element_type=F32)
            s = s[:8] + s[8:]
            fx = fx + (dx * s[4:5] - s[0:1])
            fy = fy + (dy * s[4:5] - s[1:2])
            fz = fz + (dz * s[4:5] - s[2:3])
        scale = jnp.where(lane < count_ref[i], 24.0 / 128.0, 0.0)
        force_ref[0, pl.ds(c, 1), :] = fx * scale
        force_ref[1, pl.ds(c, 1), :] = fy * scale
        force_ref[2, pl.ds(c, 1), :] = fz * scale
        return carry

    lax.fori_loop(0, 32, one, 0)


VM = pl.BlockSpec(memory_space=pltpu.VMEM)
SM = pl.BlockSpec(memory_space=pltpu.SMEM)


def density(pos, counts, flags):
    return pl.pallas_call(
        density_kernel,
        out_shape=jax.ShapeDtypeStruct((32, 128), F32),
        in_specs=[VM, SM, SM],
        out_specs=VM,
        scratch_shapes=[pltpu.VMEM((64, 128, DEPTH), BF16)],
    )(pos, counts, flags)


def force(pos, counts, flags, embed):
    return pl.pallas_call(
        force_kernel,
        out_shape=jax.ShapeDtypeStruct((3, 32, 128), F32),
        in_specs=[VM, SM, SM, VM],
        out_specs=VM,
        scratch_shapes=[pltpu.VMEM((64, 128, DEPTH), BF16), pltpu.VMEM((64, 16, 128), BF16)],
    )(pos, counts, flags, embed)


def ring(size):
    forward = [(i, (i + 1) % size) for i in range(size)]
    backward = [(i, (i - 1) % size) for i in range(size)]
    return forward, backward


def widen(block, dim, forward, backward):
    half = block.shape[dim] // 2
    low = lax.ppermute(lax.slice_in_dim(block, half, None, axis=dim), "space", forward)
    high = lax.ppermute(lax.slice_in_dim(block, 0, half, axis=dim), "space", backward)
    return jnp.concatenate([low, block, high], axis=dim)


def body(positions, velocities, thermal_noise, counts, pair_flags, exit_replica):
    forward, backward = ring(lax.axis_size("space"))
    start_pos = positions.reshape(3, 32, 128)
    noise = thermal_noise.reshape(3, 32, 128)
    own_counts = counts.reshape(32)
    tables = widen(jnp.concatenate([own_counts[None], pair_flags.reshape(13, 32)], axis=0), 1, forward, backward)
    wide_counts, wide_flags = tables[0], tables[1:]
    occupied = (jnp.arange(128, dtype=jnp.int32) < own_counts[:, None]).astype(F32)[None]
    motion = velocities.reshape(3, 32, 128) * occupied
    wide_pos = widen(start_pos, 1, forward, backward)
    coords = start_pos
    for step in range(QUENCH):
        embed = density(wide_pos, wide_counts, wide_flags)
        wide_embed = widen(embed, 0, forward, backward)
        forces = force(wide_pos, wide_counts, wide_flags, wide_embed)
        motion = motion + STEP_SIZE * forces
        if step == 0:
            mine = lax.axis_index("rep") == exit_replica[0]
            shared = jnp.stack([start_pos, motion])
            shared = lax.psum(jnp.where(mine, shared, jnp.zeros_like(shared)), "rep")
        sums = lax.psum(jnp.stack([jnp.sum(motion * motion), jnp.sum(forces * forces)]), "space")
        mixing = jnp.sqrt(sums[0] / (sums[1] + EPSILON))
        if step == 0:
            wide = widen(jnp.concatenate([motion, forces], axis=0), 1, forward, backward)
            wide_motion = (1.0 - ALPHA_MIX) * wide[:3] + ALPHA_MIX * mixing * wide[3:]
            wide_pos = wide_pos + STEP_SIZE * wide_motion
        motion = (1.0 - ALPHA_MIX) * motion + ALPHA_MIX * mixing * forces
        coords = coords + STEP_SIZE * motion
    exit_pos, exit_motion = shared[0], shared[1]
    exit_motion = FRICTION * exit_motion + KICK_SCALE * occupied * noise
    exit_pos = exit_pos + STEP_SIZE * exit_motion
    return tuple(a.reshape(positions.shape) for a in (coords, motion, exit_pos, exit_motion))


def solution(mesh):
    atoms = P("rep", None, "space", None, None, None)
    placed = (
        atoms,
        atoms,
        P("rep", None, None, "space", None, None, None),
        P("space", None, None),
        P(None, "space", None, None),
        P(),
    )
    return jax.shard_map(body, mesh=mesh, in_specs=placed, out_specs=(atoms,) * 4, check_vma=False)
```

```python
import functools
import math

import jax
import jax.numpy as jnp
from jax import lax
from jax.experimental import pallas as pl
from jax.experimental.pallas import tpu as pltpu
from jax.sharding import PartitionSpec as P

QUENCH = 2
STEP_SIZE = 0.1
ALPHA_MIX = 0.25
EPSILON = 1e-06
FRICTION = math.exp(-0.2)
KICK_SCALE = math.sqrt(1.0 - FRICTION * FRICTION)

HALF_OFFSETS = (
    [(1, p, q) for p in (-1, 0, 1) for q in (-1, 0, 1)]
    + [(0, 1, q) for q in (-1, 0, 1)]
    + [(0, 0, 1)]
)
OFFSETS = [(p, q, r) for p in (-1, 0, 1) for q in (-1, 0, 1) for r in (-1, 0, 1)]
FAR = -1.0e6
LEFT = (0, 1, 2, 0, 1, 0)
RIGHT = (0, 0, 0, 1, 1, 2)
DEPTH = 48
CHUNK = 128
UNROLL = 8
F32, BF16 = jnp.float32, jnp.bfloat16


def flag_lookup(o):
    if o in HALF_OFFSETS:
        return HALF_OFFSETS.index(o), True
    return HALF_OFFSETS.index((-o[0], -o[1], -o[2])), False


def pieces(v):
    p1 = v.astype(BF16).astype(F32)
    r = v - p1
    p2 = r.astype(BF16).astype(F32)
    return p1, p2, r - p2


def split_rows(v, order):
    p = pieces(v)
    return jnp.concatenate([p[i] for i in order], axis=0)


def prepare_partners(pos_ref, count_ref, embed_ref, left_ref, spread_ref):
    lane = lax.broadcasted_iota(jnp.int32, (1, 128), 1)
    ones = jnp.ones((1, 128), F32)
    zeros = jnp.zeros((1, 128), F32)

    def one(j, carry):
        x = pos_ref[0, pl.ds(j, 1), :]
        y = pos_ref[1, pl.ds(j, 1), :]
        z = pos_ref[2, pl.ds(j, 1), :]
        live = lane < count_ref[j]
        norm = jnp.where(live, -(x * x + y * y + z * z), FAR)
        x = jnp.where(live, x, 0.0)
        y = jnp.where(live, y, 0.0)
        z = jnp.where(live, z, 0.0)
        e = zeros if embed_ref is None else jnp.where(live, embed_ref[pl.ds(j, 1), :], 0.0)
        v = jnp.concatenate([x, y, z, norm, ones, e, zeros, zeros], axis=0)
        p = pieces(v)
        rows = [p[i] for i in LEFT]
        if spread_ref is not None:
            rows.append(v)
        table = jnp.concatenate(rows, axis=0).T
        left_ref[j] = table[:, :DEPTH].astype(BF16)
        if spread_ref is not None:
            for k in range(3):
                spread_ref[j, k] = jnp.broadcast_to(table[:, DEPTH + k : DEPTH + k + 1], (128, 128))
        return carry

    lax.fori_loop(0, 64, one, 0, unroll=UNROLL)


def centre(pos_ref, i, off_ref):
    rows = [pos_ref[k, pl.ds(i, 1), :] for k in range(3)]
    ones = jnp.ones((1, 128), F32)
    base = jnp.concatenate([2.0 * a for a in rows] + [ones, jnp.zeros((4, 128), F32)], axis=0)
    own = jnp.ones((32, 128), F32)
    for k in range(3):
        gap = rows[k] - off_ref[k]
        own = own - gap * gap
    return rows, base, own


def column(o, extra=0.0):
    row = lax.broadcasted_iota(jnp.int32, (8, 128), 0)
    col = jnp.zeros((8, 128), F32)
    for k in range(3):
        if o[k]:
            col = jnp.where(row == k, -2.0 * o[k], col)
    if extra:
        col = jnp.where(row == 5, extra, col)
    return col


def fill_offsets(off_ref):
    row = lax.broadcasted_iota(jnp.int32, (32, 128), 0)
    third = ((row // 9) - 1, (row // 3) % 3 - 1, row % 3 - 1)
    for k in range(3):
        off_ref[k] = third[k].astype(F32)


def place(c, d):
    cp, cy, cz = c // 16, (c // 4) & 3, c & 3
    return (cp + 1 + d[0]) * 16 + ((cy + d[1] + 4) & 3) * 4 + ((cz + d[2] + 4) & 3)


def flagged(flag_ref, i, j, o, own):
    if o == (0, 0, 0):
        return own
    h, forward = flag_lookup(o)
    flag = flag_ref[h, i] if forward else flag_ref[h, j]
    return jnp.where(flag > 0, own, FAR)


def not_self(t, first):
    rows = lax.broadcasted_iota(jnp.int32, t.shape, 0) + first
    cols = lax.broadcasted_iota(jnp.int32, t.shape, 1)
    return jnp.where(rows == cols, 0.0, t)


def fold(a):
    return jnp.sum(a.reshape(a.shape[0] // 8, 8, 128), axis=0)


def density_kernel(pos_ref, count_ref, flag_ref, embed_ref, left_ref, off_ref):
    prepare_partners(pos_ref, count_ref, None, left_ref, None)
    fill_offsets(off_ref)
    fifth = lax.broadcasted_iota(jnp.int32, (8, 128), 0) == 4

    def one(q, carry):
        c0 = 2 * q
        sets = [centre(pos_ref, c0 + 16 + k, off_ref) for k in (0, 1)]
        totals = [jnp.zeros((8, 128), F32), jnp.zeros((8, 128), F32)]
        for ox in (-1, 0, 1):
            for oy in (-1, 0, 1):
                for dz in (-1, 0, 1, 2):
                    j = place(c0, (ox, oy, dz))
                    used = [k for k in (0, 1) if -1 <= dz - k <= 1]
                    ws = []
                    for k in used:
                        o = (ox, oy, dz - k)
                        n = OFFSETS.index(o)
                        own = flagged(flag_ref, c0 + 16 + k, j, o, sets[k][2][n : n + 1])
                        ws.append(jnp.where(fifth, own, sets[k][1] + column(o)))
                    right = jnp.concatenate([split_rows(w, RIGHT) for w in ws], axis=1).astype(BF16)
                    for first in range(0, 128, CHUNK):
                        m = jnp.dot(left_ref[j, first : first + CHUNK], right, preferred_element_type=F32)
                        for n, k in enumerate(used):
                            t = jnp.maximum(m[:, 128 * n : 128 * n + 128], 0.0)
                            if (ox, oy, dz) == (0, 0, k):
                                t = not_self(t, first)
                            totals[k] = totals[k] + fold(t * t * t)
        for k in (0, 1):
            density = jnp.sum(totals[k], axis=0, keepdims=True) / 128.0
            embed_ref[pl.ds(c0 + k, 1), :] = -0.25 * lax.rsqrt(1.0 + density)
        return carry

    lax.fori_loop(0, 16, one, 0)


def force_kernel(pos_ref, count_ref, flag_ref, embed_ref, force_ref, left_ref, spread_ref, off_ref):
    prepare_partners(pos_ref, count_ref, embed_ref, left_ref, spread_ref)
    fill_offsets(off_ref)
    lane = lax.broadcasted_iota(jnp.int32, (1, 128), 1)
    fifth = lax.broadcasted_iota(jnp.int32, (8, 128), 0) == 4

    def one(c, carry):
        i = c + 16
        rows, base, owns = centre(pos_ref, i, off_ref)
        e = embed_ref[pl.ds(i, 1), :]
        total = [jnp.zeros((8, 128), F32) for _ in range(3)]
        for n, o in enumerate(OFFSETS):
            j = place(c, o)
            own = flagged(flag_ref, i, j, o, owns[n : n + 1])
            w = jnp.where(fifth, own, base + column(o))
            u = jnp.where(fifth, own + e, base + column(o, 1.0))
            right = jnp.concatenate([split_rows(w, RIGHT), split_rows(u, RIGHT)], axis=1).astype(BF16)
            amount = jnp.zeros((8, 128), F32)
            for first in range(0, 128, CHUNK):
                both = jnp.dot(left_ref[j, first : first + CHUNK], right, preferred_element_type=F32)
                t = jnp.maximum(both[:, :128], 0.0)
                if o == (0, 0, 0):
                    t = not_self(t, first)
                g = t * t * both[:, 128:]
                amount = amount + fold(g)
                for k in range(3):
                    total[k] = total[k] - fold(g * spread_ref[j, k, first : first + CHUNK])
            for k in range(3):
                total[k] = total[k] + (rows[k] - o[k]) * amount
        scale = jnp.where(lane < count_ref[i], 24.0 / 128.0, 0.0)
        for k in range(3):
            force_ref[k, pl.ds(c, 1), :] = jnp.sum(total[k], axis=0, keepdims=True) * scale
        return carry

    lax.fori_loop(0, 32, one, 0)


VM = pl.BlockSpec(memory_space=pltpu.VMEM)
SM = pl.BlockSpec(memory_space=pltpu.SMEM)


def density(pos, counts, flags):
    return pl.pallas_call(
        density_kernel,
        out_shape=jax.ShapeDtypeStruct((32, 128), F32),
        in_specs=[VM, SM, SM],
        out_specs=VM,
        scratch_shapes=[pltpu.VMEM((64, 128, DEPTH), BF16), pltpu.VMEM((3, 32, 128), F32)],
        compiler_params=pltpu.CompilerParams(vmem_limit_bytes=40 << 20),
        cost_estimate=pl.CostEstimate(flops=20_000_000_000, bytes_accessed=200_000, transcendentals=0),
    )(pos, counts, flags)


def force(pos, counts, flags, embed):
    return pl.pallas_call(
        force_kernel,
        out_shape=jax.ShapeDtypeStruct((3, 32, 128), F32),
        in_specs=[VM, SM, SM, VM],
        out_specs=VM,
        scratch_shapes=[
            pltpu.VMEM((64, 128, DEPTH), BF16),
            pltpu.VMEM((64, 3, 128, 128), F32),
            pltpu.VMEM((3, 32, 128), F32),
        ],
        compiler_params=pltpu.CompilerParams(vmem_limit_bytes=40 << 20),
        cost_estimate=pl.CostEstimate(flops=40_000_000_000, bytes_accessed=200_000, transcendentals=0),
    )(pos, counts, flags, embed)


MESH = pl.DeviceIdType.MESH


def peer(place):
    return (lax.axis_index("rep"), place)


def greet(places):
    barrier = pltpu.get_barrier_semaphore()
    for place in places:
        pl.semaphore_signal(barrier, inc=1, device_id=peer(place), device_id_type=MESH)
    pl.semaphore_wait(barrier, len(places))


def remote(source, target, send_sem, recv_sem, place):
    return pltpu.make_async_remote_copy(
        src_ref=source,
        dst_ref=target,
        send_sem=send_sem,
        recv_sem=recv_sem,
        device_id=peer(place),
        device_id_type=MESH,
    )


def sides(size):
    me = lax.axis_index("space")
    return lax.rem(me + size - 1, size), lax.rem(me + 1, size)


def start_kernel(size, pos_ref, table_ref, wide_ref, tables_ref, low_pos, high_pos, send_sem, recv_sem):
    left, right = sides(size)
    greet((left, right))
    copies = (
        remote(pos_ref.at[:, pl.ds(16, 16), :], low_pos, send_sem.at[0], recv_sem.at[0], right),
        remote(pos_ref.at[:, pl.ds(0, 16), :], high_pos, send_sem.at[1], recv_sem.at[1], left),
        remote(table_ref, tables_ref.at[0], send_sem.at[2], recv_sem.at[2], right),
        remote(table_ref, tables_ref.at[2], send_sem.at[3], recv_sem.at[3], left),
    )
    for copy in copies:
        copy.start()
    wide_ref[:, 16:48, :] = pos_ref[...]
    tables_ref[1] = table_ref[...]
    for copy in copies:
        copy.wait()
    wide_ref[:, 0:16, :] = low_pos[...]
    wide_ref[:, 48:64, :] = high_pos[...]


def embed_kernel(size, embed_ref, wide_ref, low, high, send_sem, recv_sem):
    left, right = sides(size)
    greet((left, right))
    copies = (
        remote(embed_ref.at[pl.ds(16, 16), :], low, send_sem.at[0], recv_sem.at[0], right),
        remote(embed_ref.at[pl.ds(0, 16), :], high, send_sem.at[1], recv_sem.at[1], left),
    )
    for copy in copies:
        copy.start()
    wide_ref[16:48, :] = embed_ref[...]
    for copy in copies:
        copy.wait()
    wide_ref[0:16, :] = low[...]
    wide_ref[48:64, :] = high[...]


def squares(a):
    return jnp.sum(jnp.sum(a * a, axis=0), axis=0, keepdims=True)


def mix_kernel(size, last, vel_ref, force_ref, wide_ref, new_pos_ref, new_vel_ref, part, slots, low, high, send_sem, recv_sem):
    me = lax.axis_index("space")
    places = [lax.rem(me + shift, size) for shift in range(1, size)]
    left, right = places[-1], places[0]
    motion, forces = vel_ref[...], force_ref[...]
    part[...] = jnp.concatenate([squares(motion), squares(forces), jnp.zeros((6, 128), F32)], axis=0)
    greet(places)
    copies = [
        remote(part, slots.at[shift], send_sem.at[shift], recv_sem.at[shift], place)
        for shift, place in enumerate(places)
    ]
    if not last:
        for k, source in enumerate((vel_ref, force_ref)):
            copies.append(
                remote(source.at[:, pl.ds(16, 16), :], low.at[k], send_sem.at[size + 2 * k], recv_sem.at[size + 2 * k], right)
            )
            copies.append(
                remote(source.at[:, pl.ds(0, 16), :], high.at[k], send_sem.at[size + 2 * k + 1], recv_sem.at[size + 2 * k + 1], left)
            )
    for copy in copies:
        copy.start()
    for copy in copies:
        copy.wait()
    total = part[...]
    for shift in range(size - 1):
        total = total + slots[shift]
    total = jnp.sum(total, axis=1, keepdims=True)
    mixing = ALPHA_MIX * jnp.sqrt(total[0:1] / (total[1:2] + EPSILON))
    mixing = mixing[None]
    new = (1.0 - ALPHA_MIX) * motion + mixing * forces
    new_vel_ref[...] = new
    moved = wide_ref[:, 16:48, :] + STEP_SIZE * new
    if last:
        new_pos_ref[...] = moved
    else:
        new_pos_ref[:, 16:48, :] = moved
        for k, (face, rows) in enumerate(((low, slice(0, 16)), (high, slice(48, 64)))):
            vel = (1.0 - ALPHA_MIX) * face[0] + mixing * face[1]
            new_pos_ref[:, rows, :] = wide_ref[:, rows, :] + STEP_SIZE * vel


def comm_params(ident):
    return pltpu.CompilerParams(collective_id=ident, has_side_effects=True)


def shaped(*shape, dtype=F32):
    return jax.ShapeDtypeStruct(shape, dtype)


def start_halo(size, pos, table):
    return pl.pallas_call(
        functools.partial(start_kernel, size),
        out_shape=(shaped(3, 64, 128), shaped(3, *table.shape, dtype=jnp.int32)),
        in_specs=[VM, VM],
        out_specs=(VM, VM),
        scratch_shapes=[
            pltpu.VMEM((3, 16, 128), F32),
            pltpu.VMEM((3, 16, 128), F32),
            pltpu.SemaphoreType.DMA((4,)),
            pltpu.SemaphoreType.DMA((4,)),
        ],
        compiler_params=comm_params(1),
    )(pos, table)


def embed_halo(size, embed):
    return pl.pallas_call(
        functools.partial(embed_kernel, size),
        out_shape=shaped(64, 128),
        in_specs=[VM],
        out_specs=VM,
        scratch_shapes=[
            pltpu.VMEM((16, 128), F32),
            pltpu.VMEM((16, 128), F32),
            pltpu.SemaphoreType.DMA((2,)),
            pltpu.SemaphoreType.DMA((2,)),
        ],
        compiler_params=comm_params(2),
    )(embed)


def mix(size, last, motion, forces, wide_pos):
    return pl.pallas_call(
        functools.partial(mix_kernel, size, last),
        out_shape=(shaped(3, 32 if last else 64, 128), shaped(3, 32, 128)),
        in_specs=[VM, VM, VM],
        out_specs=(VM, VM),
        scratch_shapes=[
            pltpu.VMEM((8, 128), F32),
            pltpu.VMEM((size - 1, 8, 128), F32),
            pltpu.VMEM((2, 3, 16, 128), F32),
            pltpu.VMEM((2, 3, 16, 128), F32),
            pltpu.SemaphoreType.DMA((size + 4,)),
            pltpu.SemaphoreType.DMA((size + 4,)),
        ],
        compiler_params=comm_params(3 + int(last)),
    )(motion, forces, wide_pos)


def gather_four(value, stage):
    size = lax.axis_size("rep")
    arrived = [lax.ppermute(value, "rep", [(i, i ^ (stage * k)) for i in range(size)]) for k in (1, 2, 3)]
    return value + arrived[0] + arrived[1] + arrived[2]


def body(positions, velocities, thermal_noise, counts, pair_flags, exit_replica):
    size = lax.axis_size("space")
    mine = lax.axis_index("rep") == exit_replica[0]
    start_pos = positions.reshape(3, 32, 128)
    noise = thermal_noise.reshape(3, 32, 128)
    own_counts = counts.reshape(32)
    table = jnp.concatenate([own_counts[None], pair_flags.reshape(13, 32)], axis=0)
    table = jnp.pad(table, ((0, 2), (0, 96)))
    wide_pos, tables = start_halo(size, start_pos, table)
    tables = jnp.concatenate([tables[0, :14, 16:32], tables[1, :14, :32], tables[2, :14, :16]], axis=1)
    wide_counts, wide_flags = tables[0], tables[1:]
    occupied = (jnp.arange(128, dtype=jnp.int32) < own_counts[:, None]).astype(F32)[None]
    motion = velocities.reshape(3, 32, 128) * occupied
    for step in range(QUENCH):
        last = step == QUENCH - 1
        embed = density(wide_pos, wide_counts, wide_flags)
        if last:
            shared = gather_four(shared, 1)
            embed, shared = lax.optimization_barrier((embed, shared))
        wide_embed = embed_halo(size, embed)
        forces = force(wide_pos, wide_counts, wide_flags, wide_embed)
        if last:
            shared = gather_four(shared, 4)
            forces, shared = lax.optimization_barrier((forces, shared))
        motion = motion + STEP_SIZE * forces
        if not last:
            shared = jnp.concatenate([start_pos, motion], axis=0)
            shared = jnp.where(mine, shared, jnp.zeros_like(shared))
        wide_pos, motion = mix(size, last, motion, forces, wide_pos)
    exit_motion = FRICTION * shared[3:] + KICK_SCALE * occupied * noise
    exit_pos = shared[:3] + STEP_SIZE * exit_motion
    return tuple(a.reshape(positions.shape) for a in (wide_pos, motion, exit_pos, exit_motion))


def solution(mesh):
    atoms = P("rep", None, "space", None, None, None)
    placed = (
        atoms,
        atoms,
        P("rep", None, None, "space", None, None, None),
        P("space", None, None),
        P(None, "space", None, None),
        P(),
    )
    return jax.shard_map(body, mesh=mesh, in_specs=placed, out_specs=(atoms,) * 4, check_vma=False)
```

```python
import functools
import math

import jax
import jax.numpy as jnp
from jax import lax
from jax.experimental import pallas as pl
from jax.experimental.pallas import tpu as pltpu
from jax.sharding import PartitionSpec as P

QUENCH = 2
STEP_SIZE = 0.1
ALPHA_MIX = 0.25
EPSILON = 1e-06
FRICTION = math.exp(-0.2)
KICK_SCALE = math.sqrt(1.0 - FRICTION * FRICTION)
HALF_OFFSETS = (
    [(1, p, q) for p in (-1, 0, 1) for q in (-1, 0, 1)]
    + [(0, 1, q) for q in (-1, 0, 1)]
    + [(0, 0, 1)]
)
OFFSETS = [(p, q, r) for p in (-1, 0, 1) for q in (-1, 0, 1) for r in (-1, 0, 1)]
FAR = -1.0e6
LEFT = (0, 1, 2, 0, 1, 0)
RIGHT = (0, 0, 0, 1, 1, 2)
DEPTH = 48
CHUNK = 128
REP_HOPS = (1, 2, 3, 4, 8, 12)
F32, BF16 = jnp.float32, jnp.bfloat16
MESH = pl.DeviceIdType.MESH


def flag_lookup(o):
    if o in HALF_OFFSETS:
        return HALF_OFFSETS.index(o), True
    return HALF_OFFSETS.index((-o[0], -o[1], -o[2])), False


def pieces(v):
    p1 = v.astype(BF16).astype(F32)
    r = v - p1
    p2 = r.astype(BF16).astype(F32)
    return p1, p2, r - p2


def split_rows(v, order):
    p = pieces(v)
    return jnp.concatenate([p[i] for i in order], axis=0)


def across(rep, hop):
    for bit in (1, 2, 4, 8):
        if hop & bit:
            rep = rep + bit - 2 * bit * lax.rem(lax.div(rep, bit), 2)
    return rep


def fold(a):
    return jnp.sum(a.reshape(a.shape[0] // 8, 8, 128), axis=0)


def squares(a):
    return jnp.sum(jnp.sum(a * a, axis=0), axis=0, keepdims=True)


def fill_constants(off_ref, pick_ref):
    row = lax.broadcasted_iota(jnp.int32, (32, 128), 0)
    third = (lax.div(row, 9) - 1, lax.rem(lax.div(row, 3), 3) - 1, lax.rem(row, 3) - 1)
    for k in range(3):
        off_ref[k] = third[k].astype(F32)
    row = lax.broadcasted_iota(jnp.int32, (DEPTH, 128), 0)
    for k in range(3):
        hit = (row == k) | (row == 8 + k) | (row == 16 + k)
        pick_ref[:, 128 * k : 128 * k + 128] = jnp.where(hit, 1.0, 0.0).astype(BF16)


def prepare_positions(pos_ref, tab_ref, left_ref, spread_ref, pick_ref):
    lane = lax.broadcasted_iota(jnp.int32, (1, 128), 1)
    ones = jnp.ones((1, 128), F32)
    zeros = jnp.zeros((3, 128), F32)

    def one(j, carry):
        live = lane < tab_ref[0, j]
        rows = [jnp.where(live, pos_ref[k, pl.ds(j, 1), :], 0.0) for k in range(3)]
        norm = jnp.where(live, -(rows[0] * rows[0] + rows[1] * rows[1] + rows[2] * rows[2]), FAR)
        v = jnp.concatenate(rows + [norm, ones, zeros], axis=0)
        left = split_rows(v, LEFT).T.astype(BF16)
        left_ref[j] = left
        spread = jnp.dot(left, pick_ref[...], preferred_element_type=F32)
        for k in range(3):
            spread_ref[j, k] = spread[:, 128 * k : 128 * k + 128]
        return carry

    lax.fori_loop(0, 64, one, 0, unroll=8)


def prepare_embed(first, count, emb_ref, left_ref):
    row = lax.broadcasted_iota(jnp.int32, (8, 128), 0)
    zeros = jnp.zeros((DEPTH - 24, 128), F32)

    def one(n, carry):
        j = first + n
        v = jnp.where(row == 5, emb_ref[pl.ds(j, 1), :], 0.0)
        table = jnp.concatenate([*pieces(v), zeros], axis=0)
        left_ref[j] = (left_ref[j].astype(F32) + table.T).astype(BF16)
        return carry

    lax.fori_loop(0, count, one, 0, unroll=8)


def centre(pos_ref, i, off_ref):
    rows = [pos_ref[k, pl.ds(i, 1), :] for k in range(3)]
    ones = jnp.ones((1, 128), F32)
    base = jnp.concatenate([2.0 * a for a in rows] + [ones, jnp.zeros((4, 128), F32)], axis=0)
    own = jnp.ones((32, 128), F32)
    for k in range(3):
        gap = rows[k] - off_ref[k]
        own = own - gap * gap
    return rows, base, own


def column(o, extra=0.0):
    row = lax.broadcasted_iota(jnp.int32, (8, 128), 0)
    col = jnp.zeros((8, 128), F32)
    for k in range(3):
        if o[k]:
            col = jnp.where(row == k, -2.0 * o[k], col)
    if extra:
        col = jnp.where(row == 5, extra, col)
    return col


def place(c, d):
    cp, cy, cz = lax.div(c, 16), lax.rem(lax.div(c, 4), 4), lax.rem(c, 4)
    return (cp + 1 + d[0]) * 16 + lax.rem(cy + d[1] + 4, 4) * 4 + lax.rem(cz + d[2] + 4, 4)


def flagged(tab_ref, i, j, o, own):
    if o == (0, 0, 0):
        return own
    h, forward = flag_lookup(o)
    flag = tab_ref[1 + h, i] if forward else tab_ref[1 + h, j]
    return jnp.where(flag > 0, own, FAR)


def not_self(t, first):
    rows = lax.broadcasted_iota(jnp.int32, t.shape, 0) + first
    cols = lax.broadcasted_iota(jnp.int32, t.shape, 1)
    return jnp.where(rows == cols, 0.0, t)


def density_pass(pos_ref, tab_ref, emb_ref, left_ref, off_ref):
    fifth = lax.broadcasted_iota(jnp.int32, (8, 128), 0) == 4

    def one(q, carry):
        c0 = 2 * q
        sets = [centre(pos_ref, c0 + 16 + k, off_ref) for k in (0, 1)]
        totals = [jnp.zeros((8, 128), F32), jnp.zeros((8, 128), F32)]
        for ox in (-1, 0, 1):
            for oy in (-1, 0, 1):
                for dz in (-1, 0, 1, 2):
                    j = place(c0, (ox, oy, dz))
                    used = [k for k in (0, 1) if -1 <= dz - k <= 1]
                    ws = []
                    for k in used:
                        o = (ox, oy, dz - k)
                        n = OFFSETS.index(o)
                        own = flagged(tab_ref, c0 + 16 + k, j, o, sets[k][2][n : n + 1])
                        ws.append(jnp.where(fifth, own, sets[k][1] + column(o)))
                    right = jnp.concatenate([split_rows(w, RIGHT) for w in ws], axis=1).astype(BF16)
                    for first in range(0, 128, CHUNK):
                        m = jnp.dot(left_ref[j, first : first + CHUNK], right, preferred_element_type=F32)
                        for n, k in enumerate(used):
                            t = jnp.maximum(m[:, 128 * n : 128 * n + 128], 0.0)
                            if (ox, oy, dz) == (0, 0, k):
                                t = not_self(t, first)
                            totals[k] = totals[k] + fold(t * t * t)
        for k in (0, 1):
            density = jnp.sum(totals[k], axis=0, keepdims=True) / 128.0
            emb_ref[pl.ds(c0 + 16 + k, 1), :] = -0.25 * lax.rsqrt(1.0 + density)
        return carry

    lax.fori_loop(0, 16, one, 0)


def force_pass(pos_ref, tab_ref, emb_ref, force_ref, left_ref, spread_ref, off_ref):
    lane = lax.broadcasted_iota(jnp.int32, (1, 128), 1)
    fifth = lax.broadcasted_iota(jnp.int32, (8, 128), 0) == 4

    def one(c, carry):
        i = c + 16
        rows, base, owns = centre(pos_ref, i, off_ref)
        e = emb_ref[pl.ds(i, 1), :]
        total = [jnp.zeros((8, 128), F32) for _ in range(3)]
        for n, o in enumerate(OFFSETS):
            j = place(c, o)
            own = flagged(tab_ref, i, j, o, owns[n : n + 1])
            w = jnp.where(fifth, own, base + column(o))
            u = jnp.where(fifth, own + e, base + column(o, 1.0))
            right = jnp.concatenate([split_rows(w, RIGHT), split_rows(u, RIGHT)], axis=1).astype(BF16)
            amount = jnp.zeros((8, 128), F32)
            for first in range(0, 128, CHUNK):
                both = jnp.dot(left_ref[j, first : first + CHUNK], right, preferred_element_type=F32)
                t = jnp.maximum(both[:, :128], 0.0)
                if o == (0, 0, 0):
                    t = not_self(t, first)
                g = t * t * both[:, 128:]
                amount = amount + fold(g)
                for k in range(3):
                    total[k] = total[k] - fold(g * spread_ref[j, k, first : first + CHUNK])
            for k in range(3):
                total[k] = total[k] + (rows[k] - o[k]) * amount
        scale = jnp.where(lane < tab_ref[0, i], 24.0 / 128.0, 0.0)
        for k in range(3):
            force_ref[k, pl.ds(c, 1), :] = jnp.sum(total[k], axis=0, keepdims=True) * scale
        return carry

    lax.fori_loop(0, 32, one, 0)


def each_row():
    for k in range(3):
        for cp in range(2):
            for cy in range(4):
                yield k, cp, cy, cp * 16 + cy * 4


def whole_kernel(
    size, pos_in, vel_in, noise_in, table_in, exit_in, qpos_out, qvel_out, dpos_out, dvel_out,
    pos, vel, frc, emb, left, spread, off, pick,
    pos_land, tab_land, emb_land, vf_land, part, slots, shared, relay, rep_land, noise, table, tab, send, recv, local,
):
    me, rep = lax.axis_index("space"), lax.axis_index("rep")
    places = [lax.rem(me + shift, size) for shift in range(1, size)]
    west, east = (rep, places[-1]), (rep, places[0])
    peers = [(rep, p) for p in places] + [(across(rep, hop), me) for hop in REP_HOPS]
    barrier = pltpu.get_barrier_semaphore()
    for where in peers:
        pl.semaphore_signal(barrier, inc=1, device_id=where, device_id_type=MESH)

    for k, cp, cy, r in each_row():
        pos[k, 16 + r : 20 + r, :] = pos_in[0, k, cp, cy]
    pl.semaphore_wait(barrier, len(peers))
    used = [0]

    def post(source, target, where):
        n = used[0]
        used[0] = n + 1
        copy = pltpu.make_async_remote_copy(
            src_ref=source,
            dst_ref=target,
            send_sem=send.at[n],
            recv_sem=recv.at[n],
            device_id=where,
            device_id_type=MESH,
        )
        copy.start()
        return copy

    flying = [
        post(table_in, tab_land.at[0], east),
        post(table_in, tab_land.at[1], west),
        post(pos.at[:, pl.ds(32, 16), :], pos_land.at[0], east),
        post(pos.at[:, pl.ds(16, 16), :], pos_land.at[1], west),
    ]
    fill_constants(off, pick)
    for k, cp, cy, r in each_row():
        vel[k, r : r + 4, :] = vel_in[0, k, cp, cy]
        noise[k, r : r + 4, :] = noise_in[0, 0, k, cp, cy]
    for copy in flying:
        copy.wait()
    lane = lax.broadcasted_iota(jnp.int32, (16, 128), 1)
    joined = jnp.where(lane < 16, pltpu.roll(tab_land[0], 112, 1), pltpu.roll(table_in[...], 16, 1))
    table[...] = jnp.where(lane < 48, joined, pltpu.roll(tab_land[1], 48, 1))
    fetch = pltpu.make_async_copy(table, tab, local.at[0])
    fetch.start()
    pos[:, 0:16, :] = pos_land[0]
    pos[:, 48:64, :] = pos_land[1]
    fetch.wait()

    lane = lax.broadcasted_iota(jnp.int32, (1, 128), 1)

    def mask_row(c, carry):
        live = lane < tab[0, c + 16]
        for k in range(3):
            vel[k, pl.ds(c, 1), :] = jnp.where(live, vel[k, pl.ds(c, 1), :], 0.0)
            noise[k, pl.ds(c, 1), :] = jnp.where(live, noise[k, pl.ds(c, 1), :], 0.0)
        return carry

    lax.fori_loop(0, 32, mask_row, 0, unroll=8)
    relays = []
    for step in range(QUENCH):
        last = step == QUENCH - 1
        prepare_positions(pos, tab, left, spread, pick)
        density_pass(pos, tab, emb, left, off)
        flying = [
            post(emb.at[pl.ds(32, 16), :], emb_land.at[step, 0], east),
            post(emb.at[pl.ds(16, 16), :], emb_land.at[step, 1], west),
        ]
        if last:
            for copy in relays:
                copy.wait()
            relay[...] = shared[...] + rep_land[0] + rep_land[1] + rep_land[2]
            relays = [post(relay, rep_land.at[n], (across(rep, REP_HOPS[n]), me)) for n in (3, 4, 5)]
        prepare_embed(16, 32, emb, left)
        for copy in flying:
            copy.wait()
        emb[0:16, :] = emb_land[step, 0]
        emb[48:64, :] = emb_land[step, 1]
        prepare_embed(0, 16, emb, left)
        prepare_embed(48, 16, emb, left)
        force_pass(pos, tab, emb, frc, left, spread, off)
        vel[...] = vel[...] + STEP_SIZE * frc[...]
        motion, forces = vel[...], frc[...]
        part[step] = jnp.concatenate([squares(motion), squares(forces), jnp.zeros((6, 128), F32)], axis=0)
        flying = [post(part.at[step], slots.at[step, n], (rep, p)) for n, p in enumerate(places)]
        if not last:
            for n, source in enumerate((vel, frc)):
                flying.append(post(source.at[:, pl.ds(16, 16), :], vf_land.at[0, n], east))
                flying.append(post(source.at[:, pl.ds(0, 16), :], vf_land.at[1, n], west))
            mine = jnp.where(rep == exit_in[0], 1.0, 0.0)
            shared[0:3] = pos[:, 16:48, :] * mine
            shared[3:6] = motion * mine
            relays = [post(shared, rep_land.at[n], (across(rep, REP_HOPS[n]), me)) for n in (0, 1, 2)]
        else:
            for copy in relays:
                copy.wait()
            totals = [relay[k] + rep_land[3, k] + rep_land[4, k] + rep_land[5, k] for k in range(6)]
            for k in range(3):
                kicked = FRICTION * totals[3 + k] + KICK_SCALE * noise[k]
                noise[k] = kicked
                shared[k] = totals[k] + STEP_SIZE * kicked
            for k, cp, cy, r in each_row():
                dvel_out[0, k, cp, cy] = noise[k, r : r + 4, :]
                dpos_out[0, k, cp, cy] = shared[k, r : r + 4, :]
        for copy in flying:
            copy.wait()
        total = part[step]
        for n in range(size - 1):
            total = total + slots[step, n]
        total = jnp.sum(total, axis=1, keepdims=True)
        mixing = (ALPHA_MIX * jnp.sqrt(total[0:1] / (total[1:2] + EPSILON)))[None]
        new = (1.0 - ALPHA_MIX) * motion + mixing * forces
        vel[...] = new
        pos[:, 16:48, :] = pos[:, 16:48, :] + STEP_SIZE * new
        if not last:
            for n, rows in enumerate((slice(0, 16), slice(48, 64))):
                moved = (1.0 - ALPHA_MIX) * vf_land[n, 0] + mixing * vf_land[n, 1]
                pos[:, rows, :] = pos[:, rows, :] + STEP_SIZE * moved
    for k, cp, cy, r in each_row():
        qpos_out[0, k, cp, cy] = pos[k, 16 + r : 20 + r, :]
        qvel_out[0, k, cp, cy] = vel[k, r : r + 4, :]


def body(positions, velocities, thermal_noise, counts, pair_flags, exit_replica):
    size = lax.axis_size("space")
    table = jnp.concatenate([counts.reshape(1, 32), pair_flags.reshape(13, 32)], axis=0)
    table = jnp.pad(table, ((0, 2), (0, 96)))
    vm = pl.BlockSpec(memory_space=pltpu.VMEM)
    sm = pl.BlockSpec(memory_space=pltpu.SMEM)
    copies = 4 + QUENCH * (2 + size - 1) + 4 + len(REP_HOPS)
    return pl.pallas_call(
        functools.partial(whole_kernel, size),
        out_shape=(jax.ShapeDtypeStruct(positions.shape, F32),) * 4,
        in_specs=[vm, vm, vm, vm, sm],
        out_specs=(vm,) * 4,
        scratch_shapes=[
            pltpu.VMEM((3, 64, 128), F32),
            pltpu.VMEM((3, 32, 128), F32),
            pltpu.VMEM((3, 32, 128), F32),
            pltpu.VMEM((64, 128), F32),
            pltpu.VMEM((64, 128, DEPTH), BF16),
            pltpu.VMEM((64, 3, 128, 128), F32),
            pltpu.VMEM((3, 32, 128), F32),
            pltpu.VMEM((DEPTH, 384), BF16),
            pltpu.VMEM((2, 3, 16, 128), F32),
            pltpu.VMEM((2, 16, 128), jnp.int32),
            pltpu.VMEM((QUENCH, 2, 16, 128), F32),
            pltpu.VMEM((2, 2, 3, 16, 128), F32),
            pltpu.VMEM((QUENCH, 8, 128), F32),
            pltpu.VMEM((QUENCH, size - 1, 8, 128), F32),
            pltpu.VMEM((6, 32, 128), F32),
            pltpu.VMEM((6, 32, 128), F32),
            pltpu.VMEM((len(REP_HOPS), 6, 32, 128), F32),
            pltpu.VMEM((3, 32, 128), F32),
            pltpu.VMEM((16, 128), jnp.int32),
            pltpu.SMEM((16, 128), jnp.int32),
            pltpu.SemaphoreType.DMA((copies,)),
            pltpu.SemaphoreType.DMA((copies,)),
            pltpu.SemaphoreType.DMA((1,)),
        ],
        compiler_params=pltpu.CompilerParams(
            collective_id=1, has_side_effects=True, vmem_limit_bytes=40 << 20
        ),
    )(positions, velocities, thermal_noise, table, exit_replica)


def solution(mesh):
    atoms = P("rep", None, "space", None, None, None)
    placed = (
        atoms,
        atoms,
        P("rep", None, None, "space", None, None, None),
        P("space", None, None),
        P(None, "space", None, None),
        P(),
    )
    return jax.shard_map(body, mesh=mesh, in_specs=placed, out_specs=(atoms,) * 4, check_vma=False)
```

```python
import functools
import math

import jax
import jax.numpy as jnp
from jax import lax
from jax.experimental import pallas as pl
from jax.experimental.pallas import tpu as pltpu
from jax.sharding import PartitionSpec as P

QUENCH = 2
STEP_SIZE = 0.1
ALPHA_MIX = 0.25
EPSILON = 1e-06
FRICTION = math.exp(-0.2)
KICK_SCALE = math.sqrt(1.0 - FRICTION * FRICTION)
HALF_OFFSETS = (
    [(1, p, q) for p in (-1, 0, 1) for q in (-1, 0, 1)]
    + [(0, 1, q) for q in (-1, 0, 1)]
    + [(0, 0, 1)]
)
OFFSETS = [(p, q, r) for p in (-1, 0, 1) for q in (-1, 0, 1) for r in (-1, 0, 1)]
FAR = -1.0e6
LEFT = (0, 1, 2, 0, 1, 0)
RIGHT = (0, 0, 0, 1, 1, 2)
DEPTH = 48
DENSITY_CELLS = 4
FORCE_CELLS = 2
REP_HOPS = (1, 2, 3, 4, 8, 12)
F32, BF16 = jnp.float32, jnp.bfloat16
MESH = pl.DeviceIdType.MESH


def flag_lookup(o):
    if o in HALF_OFFSETS:
        return HALF_OFFSETS.index(o), True
    return HALF_OFFSETS.index((-o[0], -o[1], -o[2])), False


def pieces(v):
    p1 = v.astype(BF16).astype(F32)
    r = v - p1
    p2 = r.astype(BF16).astype(F32)
    return p1, p2, r - p2


def split_rows(v, order):
    p = pieces(v)
    return jnp.concatenate([p[i] for i in order], axis=0)


def across(rep, hop):
    for bit in (1, 2, 4, 8):
        if hop & bit:
            rep = rep + bit - 2 * bit * lax.rem(lax.div(rep, bit), 2)
    return rep


def fold(a):
    return jnp.sum(a.reshape(a.shape[0] // 8, 8, 128), axis=0)


def squares(a):
    return jnp.sum(jnp.sum(a * a, axis=0), axis=0, keepdims=True)


def fill_constants(off_ref, pick_ref):
    row = lax.broadcasted_iota(jnp.int32, (32, 128), 0)
    third = (lax.div(row, 9) - 1, lax.rem(lax.div(row, 3), 3) - 1, lax.rem(row, 3) - 1)
    for k in range(3):
        off_ref[k] = third[k].astype(F32)
    row = lax.broadcasted_iota(jnp.int32, (DEPTH, 128), 0)
    for k in range(3):
        hit = (row == k) | (row == 8 + k) | (row == 16 + k)
        pick_ref[:, 128 * k : 128 * k + 128] = jnp.where(hit, 1.0, 0.0).astype(BF16)


def prepare_positions(pos_ref, tab_ref, left_ref, spread_ref, pick_ref):
    lane = lax.broadcasted_iota(jnp.int32, (1, 128), 1)
    ones = jnp.ones((1, 128), F32)
    zeros = jnp.zeros((3, 128), F32)

    def one(j, carry):
        live = lane < tab_ref[0, j]
        rows = [jnp.where(live, pos_ref[k, pl.ds(j, 1), :], 0.0) for k in range(3)]
        norm = jnp.where(live, -(rows[0] * rows[0] + rows[1] * rows[1] + rows[2] * rows[2]), FAR)
        v = jnp.concatenate(rows + [norm, ones, zeros], axis=0)
        left = split_rows(v, LEFT).T.astype(BF16)
        left_ref[j] = left
        spread = jnp.dot(left, pick_ref[...], preferred_element_type=F32)
        for k in range(3):
            spread_ref[j, k] = spread[:, 128 * k : 128 * k + 128]
        return carry

    lax.fori_loop(0, 64, one, 0, unroll=8)


def prepare_embed(first, count, emb_ref, left_ref):
    row = lax.broadcasted_iota(jnp.int32, (8, 128), 0)
    zeros = jnp.zeros((DEPTH - 24, 128), F32)

    def one(n, carry):
        j = first + n
        v = jnp.where(row == 5, emb_ref[pl.ds(j, 1), :], 0.0)
        table = jnp.concatenate([*pieces(v), zeros], axis=0)
        left_ref[j] = (left_ref[j].astype(F32) + table.T).astype(BF16)
        return carry

    lax.fori_loop(0, count, one, 0, unroll=8)


def centre(pos_ref, i, off_ref, own_ref, slot, e=None):
    rows = [pos_ref[k, pl.ds(i, 1), :] for k in range(3)]
    ones = jnp.ones((1, 128), F32)
    zeros = jnp.zeros((4, 128), F32)
    shifted = {
        v: pieces(jnp.concatenate([2.0 * (a - v) for a in rows] + [ones, zeros], axis=0)) for v in (-1, 0, 1)
    }
    own = jnp.ones((32, 128), F32)
    for k in range(3):
        gap = rows[k] - off_ref[k]
        own = own - gap * gap
    for k, part in enumerate(pieces(own)):
        own_ref[slot, k] = part
    if e is not None:
        for k, part in enumerate(pieces(own + e)):
            own_ref[slot, 3 + k] = part
    return rows, shifted


def row_masks():
    row = lax.broadcasted_iota(jnp.int32, (8, 128), 0)
    return row == 0, row < 2, row == 4


def in_plane(shifted, ox, oy, masks):
    return [jnp.where(masks[0], shifted[ox][k], shifted[oy][k]) for k in range(3)]


def order_rows(parts):
    return jnp.concatenate([parts[i] for i in RIGHT], axis=0).astype(BF16)


def right_rows(flat, shifted, o, live, own_ref, slot, masks, second=None):
    n = OFFSETS.index(o)
    parts = [jnp.where(masks[1], flat[k], shifted[o[2]][k]) for k in range(3)]
    own = [own_ref[slot, k, n : n + 1] for k in range(3)]
    if live is not None:
        own[0] = jnp.where(live, own[0], FAR)
    plain = order_rows([jnp.where(masks[2], own[k], parts[k]) for k in range(3)])
    if second is None:
        return plain
    parts[0] = parts[0] + second
    both = order_rows([jnp.where(masks[2], own_ref[slot, 3 + k, n : n + 1], parts[k]) for k in range(3)])
    return jnp.concatenate([plain, both], axis=1)


def place(c, d):
    cp, cy, cz = lax.div(c, 16), lax.rem(lax.div(c, 4), 4), lax.rem(c, 4)
    return (cp + 1 + d[0]) * 16 + lax.rem(cy + d[1] + 4, 4) * 4 + lax.rem(cz + d[2] + 4, 4)


def listed(tab_ref, i, j, o):
    if o == (0, 0, 0):
        return None
    h, forward = flag_lookup(o)
    return (tab_ref[1 + h, i] if forward else tab_ref[1 + h, j]) > 0


def not_self(t, first):
    rows = lax.broadcasted_iota(jnp.int32, t.shape, 0) + first
    cols = lax.broadcasted_iota(jnp.int32, t.shape, 1)
    return jnp.where(rows == cols, 0.0, t)


def walk(width):
    for ox in (-1, 0, 1):
        for oy in (-1, 0, 1):
            for dz in range(-1, width + 1) if width < 4 else range(4):
                used = []
                for k in range(width):
                    oz = dz - k
                    if width == 4 and abs(oz) == 3:
                        oz = -oz // 3
                    if -1 <= oz <= 1:
                        used.append((k, (ox, oy, oz)))
                yield ox, oy, dz, used


def density_pass(pos_ref, tab_ref, emb_ref, left_ref, off_ref, own_ref):
    masks = row_masks()
    width = DENSITY_CELLS

    def one(q, carry):
        c0 = width * q
        sets = [centre(pos_ref, c0 + 16 + k, off_ref, own_ref, k) for k in range(width)]
        totals = [jnp.zeros((8, 128), F32)] * width
        flats = None
        for ox, oy, dz, used in walk(width):
            if dz in (-1, 0) and used[0][1][2] == (dz if width < 4 else 0):
                flats = [in_plane(s[1], ox, oy, masks) for s in sets]
            j = place(c0, (ox, oy, dz))
            right = [
                right_rows(flats[k], sets[k][1], o, listed(tab_ref, c0 + 16 + k, j, o), own_ref, k, masks)
                for k, o in used
            ]
            m = jnp.dot(left_ref[j], jnp.concatenate(right, axis=1), preferred_element_type=F32)
            for first in range(0, 128, 8):
                for n, (k, o) in enumerate(used):
                    t = jnp.maximum(m[first : first + 8, 128 * n : 128 * n + 128], 0.0)
                    if o == (0, 0, 0):
                        t = not_self(t, first)
                    totals[k] = totals[k] + t * t * t
        for k in range(width):
            density = jnp.sum(totals[k], axis=0, keepdims=True) / 128.0
            emb_ref[pl.ds(c0 + 16 + k, 1), :] = -0.25 * lax.rsqrt(1.0 + density)
        return carry

    lax.fori_loop(0, 32 // width, one, 0)


def force_pass(pos_ref, tab_ref, emb_ref, force_ref, left_ref, spread_ref, off_ref, own_ref):
    lane = lax.broadcasted_iota(jnp.int32, (1, 128), 1)
    second = jnp.where(lax.broadcasted_iota(jnp.int32, (8, 128), 0) == 5, 1.0, 0.0)
    masks = row_masks()
    width = FORCE_CELLS

    def one(q, carry):
        c0 = width * q
        sets = [
            centre(pos_ref, c0 + 16 + k, off_ref, own_ref, k, emb_ref[pl.ds(c0 + 16 + k, 1), :])
            for k in range(width)
        ]
        total = [[jnp.zeros((8, 128), F32) for _ in range(3)] for _ in range(width)]
        flats = None
        for ox, oy, dz, used in walk(width):
            if dz in (-1, 0) and used[0][1][2] == (dz if width < 4 else 0):
                flats = [in_plane(s[1], ox, oy, masks) for s in sets]
            j = place(c0, (ox, oy, dz))
            boths, amounts = [], []
            for k, o in used:
                right = right_rows(
                    flats[k], sets[k][1], o, listed(tab_ref, c0 + 16 + k, j, o), own_ref, k, masks, second
                )
                boths.append(jnp.dot(left_ref[j], right, preferred_element_type=F32))
                amounts.append(jnp.zeros((8, 128), F32))
            for first in range(0, 128, 8):
                spread = [spread_ref[j, d, first : first + 8] for d in range(3)]
                for n, (k, o) in enumerate(used):
                    t = jnp.maximum(boths[n][first : first + 8, :128], 0.0)
                    if o == (0, 0, 0):
                        t = not_self(t, first)
                    g = t * t * boths[n][first : first + 8, 128:]
                    amounts[n] = amounts[n] + g
                    for d in range(3):
                        total[k][d] = total[k][d] - g * spread[d]
            for n, (k, o) in enumerate(used):
                for d in range(3):
                    total[k][d] = total[k][d] + (sets[k][0][d] - o[d]) * amounts[n]
        for k in range(width):
            scale = jnp.where(lane < tab_ref[0, c0 + 16 + k], 24.0 / 128.0, 0.0)
            for d in range(3):
                force_ref[d, pl.ds(c0 + k, 1), :] = jnp.sum(total[k][d], axis=0, keepdims=True) * scale
        return carry

    lax.fori_loop(0, 32 // width, one, 0)


def each_row():
    for k in range(3):
        for cp in range(2):
            for cy in range(4):
                yield k, cp, cy, cp * 16 + cy * 4


def whole_kernel(
    size, pos_in, vel_in, table_in, exit_in, pos_out, vel_out, frc_out, xpos_out, xvel_out, occ_out, mix_out,
    pos, vel, frc, emb, left, spread, off, own, pick,
    pos_land, tab_land, emb_land, vf_land, part, slots, shared, relay, rep_land, pos_copy, vel_copy, occ, table, tab, send, recv, local,
):
    me, rep = lax.axis_index("space"), lax.axis_index("rep")
    places = [lax.rem(me + shift, size) for shift in range(1, size)]
    west, east = (rep, places[-1]), (rep, places[0])
    peers = [(rep, p) for p in places] + [(across(rep, hop), me) for hop in REP_HOPS]
    barrier = pltpu.get_barrier_semaphore()
    for where in peers:
        pl.semaphore_signal(barrier, inc=1, device_id=where, device_id_type=MESH)

    loads = [
        pltpu.make_async_copy(source.at[0], target, local.at[1 + n])
        for n, (source, target) in enumerate(((pos_in, pos_copy), (vel_in, vel_copy)))
    ]
    for load in loads:
        load.start()
    fill_constants(off, pick)
    for load in loads:
        load.wait()
    for k, cp, cy, r in each_row():
        pos[k, 16 + r : 20 + r, :] = pos_copy[k, cp, cy]
        vel[k, r : r + 4, :] = vel_copy[k, cp, cy]
    pl.semaphore_wait(barrier, len(peers))
    used = [0]

    def post(source, target, where):
        n = used[0]
        used[0] = n + 1
        copy = pltpu.make_async_remote_copy(
            src_ref=source,
            dst_ref=target,
            send_sem=send.at[n],
            recv_sem=recv.at[n],
            device_id=where,
            device_id_type=MESH,
        )
        copy.start()
        return copy

    flying = [
        post(table_in, tab_land.at[0], east),
        post(table_in, tab_land.at[1], west),
        post(pos.at[:, pl.ds(32, 16), :], pos_land.at[0], east),
        post(pos.at[:, pl.ds(16, 16), :], pos_land.at[1], west),
    ]
    for copy in flying:
        copy.wait()
    lane = lax.broadcasted_iota(jnp.int32, (16, 128), 1)
    joined = jnp.where(lane < 16, pltpu.roll(tab_land[0], 112, 1), pltpu.roll(table_in[...], 16, 1))
    table[...] = jnp.where(lane < 48, joined, pltpu.roll(tab_land[1], 48, 1))
    fetch = pltpu.make_async_copy(table, tab, local.at[0])
    fetch.start()
    pos[:, 0:16, :] = pos_land[0]
    pos[:, 48:64, :] = pos_land[1]
    fetch.wait()

    lane = lax.broadcasted_iota(jnp.int32, (1, 128), 1)

    def mask_row(c, carry):
        live = lane < tab[0, c + 16]
        occ[pl.ds(c, 1), :] = jnp.where(live, KICK_SCALE, 0.0)
        for k in range(3):
            vel[k, pl.ds(c, 1), :] = jnp.where(live, vel[k, pl.ds(c, 1), :], 0.0)
        return carry

    lax.fori_loop(0, 32, mask_row, 0, unroll=8)
    relays = []
    for step in range(QUENCH):
        last = step == QUENCH - 1
        prepare_positions(pos, tab, left, spread, pick)
        density_pass(pos, tab, emb, left, off, own)
        flying = [
            post(emb.at[pl.ds(32, 16), :], emb_land.at[step, 0], east),
            post(emb.at[pl.ds(16, 16), :], emb_land.at[step, 1], west),
        ]
        if last:
            for copy in relays:
                copy.wait()
            relay[...] = shared[...] + rep_land[0] + rep_land[1] + rep_land[2]
            relays = [post(relay, rep_land.at[n], (across(rep, REP_HOPS[n]), me)) for n in (3, 4, 5)]
        prepare_embed(16, 32, emb, left)
        for copy in flying:
            copy.wait()
        emb[0:16, :] = emb_land[step, 0]
        emb[48:64, :] = emb_land[step, 1]
        prepare_embed(0, 16, emb, left)
        prepare_embed(48, 16, emb, left)
        force_pass(pos, tab, emb, frc, left, spread, off, own)
        vel[...] = vel[...] + STEP_SIZE * frc[...]
        motion, forces = vel[...], frc[...]
        part[step] = jnp.concatenate([squares(motion), squares(forces), jnp.zeros((6, 128), F32)], axis=0)
        flying = [post(part.at[step], slots.at[step, n], (rep, p)) for n, p in enumerate(places)]
        if not last:
            for n, source in enumerate((vel, frc)):
                flying.append(post(source.at[:, pl.ds(16, 16), :], vf_land.at[0, n], east))
                flying.append(post(source.at[:, pl.ds(0, 16), :], vf_land.at[1, n], west))
            mine = jnp.where(rep == exit_in[0], 1.0, 0.0)
            shared[0:3] = pos[:, 16:48, :] * mine
            shared[3:6] = motion * mine
            relays = [post(shared, rep_land.at[n], (across(rep, REP_HOPS[n]), me)) for n in (0, 1, 2)]
        else:
            for copy in relays:
                copy.wait()
            for n in range(6):
                shared[n] = relay[n] + rep_land[3, n] + rep_land[4, n] + rep_land[5, n]
            for k, cp, cy, r in each_row():
                pos_out[0, k, cp, cy] = pos[k, 16 + r : 20 + r, :]
                vel_out[0, k, cp, cy] = vel[k, r : r + 4, :]
                frc_out[0, k, cp, cy] = frc[k, r : r + 4, :]
                xpos_out[0, k, cp, cy] = shared[k, r : r + 4, :]
                xvel_out[0, k, cp, cy] = shared[3 + k, r : r + 4, :]
                if k == 0:
                    occ_out[cp, cy] = occ[r : r + 4, :]
        for copy in flying:
            copy.wait()
        total = part[step]
        for n in range(size - 1):
            total = total + slots[step, n]
        total = jnp.sum(total, axis=1, keepdims=True)
        mixing = ALPHA_MIX * jnp.sqrt(total[0:1] / (total[1:2] + EPSILON))
        if last:
            mix_out[...] = jnp.broadcast_to(mixing, (1, 128))
        else:
            mixing = mixing[None]
            new = (1.0 - ALPHA_MIX) * motion + mixing * forces
            vel[...] = new
            pos[:, 16:48, :] = pos[:, 16:48, :] + STEP_SIZE * new
            for n, rows in enumerate((slice(0, 16), slice(48, 64))):
                moved = (1.0 - ALPHA_MIX) * vf_land[n, 0] + mixing * vf_land[n, 1]
                pos[:, rows, :] = pos[:, rows, :] + STEP_SIZE * moved


def body(positions, velocities, thermal_noise, counts, pair_flags, exit_replica):
    size = lax.axis_size("space")
    table = jnp.concatenate([counts.reshape(1, 32), pair_flags.reshape(13, 32)], axis=0)
    table = jnp.pad(table, ((0, 2), (0, 96)))
    vm = pl.BlockSpec(memory_space=pltpu.VMEM)
    sm = pl.BlockSpec(memory_space=pltpu.SMEM)
    copies = 4 + QUENCH * (2 + size - 1) + 4 + len(REP_HOPS)
    pos, vel, frc, xpos, xvel, kick, mixing = pl.pallas_call(
        functools.partial(whole_kernel, size),
        out_shape=(jax.ShapeDtypeStruct(positions.shape, F32),) * 5 + (
            jax.ShapeDtypeStruct((2, 4, 4, 128), F32),
            jax.ShapeDtypeStruct((1, 128), F32),
        ),
        in_specs=[pl.BlockSpec(memory_space=pltpu.HBM)] * 2 + [vm, sm],
        out_specs=(vm,) * 7,
        scratch_shapes=[
            pltpu.VMEM((3, 64, 128), F32),
            pltpu.VMEM((3, 32, 128), F32),
            pltpu.VMEM((3, 32, 128), F32),
            pltpu.VMEM((64, 128), F32),
            pltpu.VMEM((64, 128, DEPTH), BF16),
            pltpu.VMEM((64, 3, 128, 128), F32),
            pltpu.VMEM((3, 32, 128), F32),
            pltpu.VMEM((4, 6, 32, 128), F32),
            pltpu.VMEM((DEPTH, 384), BF16),
            pltpu.VMEM((2, 3, 16, 128), F32),
            pltpu.VMEM((2, 16, 128), jnp.int32),
            pltpu.VMEM((QUENCH, 2, 16, 128), F32),
            pltpu.VMEM((2, 2, 3, 16, 128), F32),
            pltpu.VMEM((QUENCH, 8, 128), F32),
            pltpu.VMEM((QUENCH, size - 1, 8, 128), F32),
            pltpu.VMEM((6, 32, 128), F32),
            pltpu.VMEM((6, 32, 128), F32),
            pltpu.VMEM((len(REP_HOPS), 6, 32, 128), F32),
            pltpu.VMEM((3, 2, 4, 4, 128), F32),
            pltpu.VMEM((3, 2, 4, 4, 128), F32),
            pltpu.VMEM((32, 128), F32),
            pltpu.VMEM((16, 128), jnp.int32),
            pltpu.SMEM((16, 128), jnp.int32),
            pltpu.SemaphoreType.DMA((copies,)),
            pltpu.SemaphoreType.DMA((copies,)),
            pltpu.SemaphoreType.DMA((3,)),
        ],
        compiler_params=pltpu.CompilerParams(
            collective_id=1, has_side_effects=True, vmem_limit_bytes=40 << 20
        ),
    )(positions, velocities, table, exit_replica)
    quench_vel = (1.0 - ALPHA_MIX) * vel + mixing.reshape(128) * frc
    dephase_vel = FRICTION * xvel + kick * thermal_noise[0]
    return pos + STEP_SIZE * quench_vel, quench_vel, xpos + STEP_SIZE * dephase_vel, dephase_vel


def solution(mesh):
    atoms = P("rep", None, "space", None, None, None)
    placed = (
        atoms,
        atoms,
        P("rep", None, None, "space", None, None, None),
        P("space", None, None),
        P(None, "space", None, None),
        P(),
    )
    return jax.shard_map(body, mesh=mesh, in_specs=placed, out_specs=(atoms,) * 4, check_vma=False)
```

```python
import functools
import math

import jax
import jax.numpy as jnp
from jax import lax
from jax.experimental import pallas as pl
from jax.experimental.pallas import tpu as pltpu
from jax.sharding import PartitionSpec as P

QUENCH = 2
STEP_SIZE = 0.1
ALPHA_MIX = 0.25
EPSILON = 1e-06
FRICTION = math.exp(-0.2)
KICK_SCALE = math.sqrt(1.0 - FRICTION * FRICTION)
HALF_OFFSETS = (
    [(1, p, q) for p in (-1, 0, 1) for q in (-1, 0, 1)]
    + [(0, 1, q) for q in (-1, 0, 1)]
    + [(0, 0, 1)]
)
OFFSETS = [(p, q, r) for p in (-1, 0, 1) for q in (-1, 0, 1) for r in (-1, 0, 1)]
FAR = -1.0e6
LEFT = (0, 1, 2, 0, 1, 0)
RIGHT = (0, 0, 0, 1, 1, 2)
DEPTH = 48
DENSITY_CELLS = 4
FORCE_CELLS = 2
REP_HOPS = (1, 2, 3, 4, 8, 12)
F32, BF16 = jnp.float32, jnp.bfloat16
MESH = pl.DeviceIdType.MESH


def flag_lookup(o):
    if o in HALF_OFFSETS:
        return HALF_OFFSETS.index(o), True
    return HALF_OFFSETS.index((-o[0], -o[1], -o[2])), False


def pieces(v):
    p1 = v.astype(BF16).astype(F32)
    r = v - p1
    p2 = r.astype(BF16).astype(F32)
    return p1, p2, r - p2


def split_rows(v, order):
    p = pieces(v)
    return jnp.concatenate([p[i] for i in order], axis=0)


def across(rep, hop):
    for bit in (1, 2, 4, 8):
        if hop & bit:
            rep = rep + bit - 2 * bit * lax.rem(lax.div(rep, bit), 2)
    return rep


def fold(a):
    return jnp.sum(a.reshape(a.shape[0] // 8, 8, 128), axis=0)


def squares(a):
    return jnp.sum(jnp.sum(a * a, axis=0), axis=0, keepdims=True)


def fill_constants(off_ref, pick_ref):
    row = lax.broadcasted_iota(jnp.int32, (32, 128), 0)
    third = (lax.div(row, 9) - 1, lax.rem(lax.div(row, 3), 3) - 1, lax.rem(row, 3) - 1)
    for k in range(3):
        off_ref[k] = third[k].astype(F32)
    row = lax.broadcasted_iota(jnp.int32, (DEPTH, 128), 0)
    for k in range(3):
        hit = (row == k) | (row == 8 + k) | (row == 16 + k)
        pick_ref[:, 128 * k : 128 * k + 128] = jnp.where(hit, 1.0, 0.0).astype(BF16)


def prepare_positions(pos_ref, tab_ref, left_ref, spread_ref, pick_ref):
    lane = lax.broadcasted_iota(jnp.int32, (1, 128), 1)
    ones = jnp.ones((1, 128), F32)
    zeros = jnp.zeros((3, 128), F32)

    def one(j, carry):
        live = lane < tab_ref[0, j]
        rows = [jnp.where(live, pos_ref[k, pl.ds(j, 1), :], 0.0) for k in range(3)]
        norm = jnp.where(live, -(rows[0] * rows[0] + rows[1] * rows[1] + rows[2] * rows[2]), FAR)
        v = jnp.concatenate(rows + [norm, ones, zeros], axis=0)
        left = split_rows(v, LEFT).T.astype(BF16)
        left_ref[j] = left
        spread = jnp.dot(left, pick_ref[...], preferred_element_type=F32)
        for k in range(3):
            spread_ref[j, k] = spread[:, 128 * k : 128 * k + 128]
        return carry

    lax.fori_loop(0, 64, one, 0, unroll=8)


def prepare_embed(first, count, emb_ref, left_ref):
    row = lax.broadcasted_iota(jnp.int32, (8, 128), 0)
    zeros = jnp.zeros((DEPTH - 24, 128), F32)

    def one(n, carry):
        j = first + n
        v = jnp.where(row == 5, emb_ref[pl.ds(j, 1), :], 0.0)
        table = jnp.concatenate([*pieces(v), zeros], axis=0)
        left_ref[j] = (left_ref[j].astype(F32) + table.T).astype(BF16)
        return carry

    lax.fori_loop(0, count, one, 0, unroll=8)


def centre(pos_ref, i, off_ref, own_ref, slot, e=None):
    rows = [pos_ref[k, pl.ds(i, 1), :] for k in range(3)]
    ones = jnp.ones((1, 128), F32)
    zeros = jnp.zeros((4, 128), F32)
    shifted = {
        v: pieces(jnp.concatenate([2.0 * (a - v) for a in rows] + [ones, zeros], axis=0)) for v in (-1, 0, 1)
    }
    own = jnp.ones((32, 128), F32)
    for k in range(3):
        gap = rows[k] - off_ref[k]
        own = own - gap * gap
    for k, part in enumerate(pieces(own)):
        own_ref[slot, k] = part
    if e is not None:
        for k, part in enumerate(pieces(own + e)):
            own_ref[slot, 3 + k] = part
    return rows, shifted


def row_masks():
    row = lax.broadcasted_iota(jnp.int32, (8, 128), 0)
    return row == 0, row < 2, row == 4


def in_plane(shifted, ox, oy, masks):
    return [jnp.where(masks[0], shifted[ox][k], shifted[oy][k]) for k in range(3)]


def order_rows(parts):
    return jnp.concatenate([parts[i] for i in RIGHT], axis=0).astype(BF16)


def right_rows(flat, shifted, o, live, own_ref, slot, masks, second=None):
    n = OFFSETS.index(o)
    parts = [jnp.where(masks[1], flat[k], shifted[o[2]][k]) for k in range(3)]
    own = [own_ref[slot, k, n : n + 1] for k in range(3)]
    if live is not None:
        own[0] = jnp.where(live, own[0], FAR)
    plain = order_rows([jnp.where(masks[2], own[k], parts[k]) for k in range(3)])
    if second is None:
        return plain
    parts[0] = parts[0] + second
    both = order_rows([jnp.where(masks[2], own_ref[slot, 3 + k, n : n + 1], parts[k]) for k in range(3)])
    return jnp.concatenate([plain, both], axis=1)


def place(c, d):
    cp, cy, cz = lax.div(c, 16), lax.rem(lax.div(c, 4), 4), lax.rem(c, 4)
    return (cp + 1 + d[0]) * 16 + lax.rem(cy + d[1] + 4, 4) * 4 + lax.rem(cz + d[2] + 4, 4)


def listed(tab_ref, i, j, o):
    if o == (0, 0, 0):
        return None
    h, forward = flag_lookup(o)
    return (tab_ref[1 + h, i] if forward else tab_ref[1 + h, j]) > 0


def not_self(t, first):
    rows = lax.broadcasted_iota(jnp.int32, t.shape, 0) + first
    cols = lax.broadcasted_iota(jnp.int32, t.shape, 1)
    return jnp.where(rows == cols, 0.0, t)


def walk(width):
    for ox in (-1, 0, 1):
        for oy in (-1, 0, 1):
            for dz in range(-1, width + 1) if width < 4 else range(4):
                used = []
                for k in range(width):
                    oz = dz - k
                    if width == 4 and abs(oz) == 3:
                        oz = -oz // 3
                    if -1 <= oz <= 1:
                        used.append((k, (ox, oy, oz)))
                yield ox, oy, dz, used


def density_pass(pos_ref, tab_ref, emb_ref, left_ref, off_ref, own_ref):
    masks = row_masks()
    width = DENSITY_CELLS

    def one(q, carry):
        c0 = width * q
        sets = [centre(pos_ref, c0 + 16 + k, off_ref, own_ref, k) for k in range(width)]
        totals = [jnp.zeros((8, 128), F32)] * width
        flats = None
        for ox, oy, dz, used in walk(width):
            if dz in (-1, 0) and used[0][1][2] == (dz if width < 4 else 0):
                flats = [in_plane(s[1], ox, oy, masks) for s in sets]
            j = place(c0, (ox, oy, dz))
            right = [
                right_rows(flats[k], sets[k][1], o, listed(tab_ref, c0 + 16 + k, j, o), own_ref, k, masks)
                for k, o in used
            ]
            m = jnp.dot(left_ref[j], jnp.concatenate(right, axis=1), preferred_element_type=F32)
            for first in range(0, 128, 8):
                for n, (k, o) in enumerate(used):
                    t = jnp.maximum(m[first : first + 8, 128 * n : 128 * n + 128], 0.0)
                    if o == (0, 0, 0):
                        t = not_self(t, first)
                    totals[k] = totals[k] + t * t * t
        for k in range(width):
            density = jnp.sum(totals[k], axis=0, keepdims=True) / 128.0
            emb_ref[pl.ds(c0 + 16 + k, 1), :] = -0.25 * lax.rsqrt(1.0 + density)
        return carry

    lax.fori_loop(0, 32 // width, one, 0)


def force_pass(pos_ref, tab_ref, emb_ref, force_ref, left_ref, spread_ref, off_ref, own_ref):
    lane = lax.broadcasted_iota(jnp.int32, (1, 128), 1)
    second = jnp.where(lax.broadcasted_iota(jnp.int32, (8, 128), 0) == 5, 1.0, 0.0)
    masks = row_masks()
    width = FORCE_CELLS

    def one(q, carry):
        c0 = width * q
        sets = [
            centre(pos_ref, c0 + 16 + k, off_ref, own_ref, k, emb_ref[pl.ds(c0 + 16 + k, 1), :])
            for k in range(width)
        ]
        total = [[jnp.zeros((8, 128), F32) for _ in range(3)] for _ in range(width)]
        flats = None
        for ox, oy, dz, used in walk(width):
            if dz in (-1, 0) and used[0][1][2] == (dz if width < 4 else 0):
                flats = [in_plane(s[1], ox, oy, masks) for s in sets]
            j = place(c0, (ox, oy, dz))
            boths, amounts = [], []
            for k, o in used:
                right = right_rows(
                    flats[k], sets[k][1], o, listed(tab_ref, c0 + 16 + k, j, o), own_ref, k, masks, second
                )
                boths.append(jnp.dot(left_ref[j], right, preferred_element_type=F32))
                amounts.append(jnp.zeros((8, 128), F32))
            for first in range(0, 128, 8):
                spread = [spread_ref[j, d, first : first + 8] for d in range(3)]
                for n, (k, o) in enumerate(used):
                    t = jnp.maximum(boths[n][first : first + 8, :128], 0.0)
                    if o == (0, 0, 0):
                        t = not_self(t, first)
                    g = t * t * boths[n][first : first + 8, 128:]
                    amounts[n] = amounts[n] + g
                    for d in range(3):
                        total[k][d] = total[k][d] - g * spread[d]
            for n, (k, o) in enumerate(used):
                for d in range(3):
                    total[k][d] = total[k][d] + (sets[k][0][d] - o[d]) * amounts[n]
        for k in range(width):
            scale = jnp.where(lane < tab_ref[0, c0 + 16 + k], 24.0 / 128.0, 0.0)
            for d in range(3):
                force_ref[d, pl.ds(c0 + k, 1), :] = jnp.sum(total[k][d], axis=0, keepdims=True) * scale
        return carry

    lax.fori_loop(0, 32 // width, one, 0)


def each_row():
    for k in range(3):
        for cp in range(2):
            for cy in range(4):
                yield k, cp, cy, cp * 16 + cy * 4


def whole_kernel(
    size, pos_in, vel_in, table_in, exit_in, pos_out, vel_out, frc_out, xpos_out, xvel_out, occ_out, mix_out,
    pos, vel, frc, emb, left, spread, off, own, pick,
    pos_land, tab_land, emb_land, vf_land, part, slots, shared, relay, rep_land, pos_copy, vel_copy, occ, listing, table, tab, send, recv, local,
):
    me, rep = lax.axis_index("space"), lax.axis_index("rep")
    places = [lax.rem(me + shift, size) for shift in range(1, size)]
    west, east = (rep, places[-1]), (rep, places[0])
    peers = [(rep, p) for p in places] + [(across(rep, hop), me) for hop in REP_HOPS]
    barrier = pltpu.get_barrier_semaphore()
    for where in peers:
        pl.semaphore_signal(barrier, inc=1, device_id=where, device_id_type=MESH)

    loads = [
        pltpu.make_async_copy(source.at[0], target, local.at[1 + n])
        for n, (source, target) in enumerate(((pos_in, pos_copy), (vel_in, vel_copy)))
    ]
    for load in loads:
        load.start()
    fill_constants(off, pick)
    stack = jnp.concatenate([table_in[cp, cy] for cp in range(2) for cy in range(4)], axis=0).astype(F32)
    stack = jnp.concatenate([stack, jnp.zeros((96, 128), F32)], axis=0).T
    listing[...] = stack[:16].astype(jnp.int32)
    for load in loads:
        load.wait()
    for k, cp, cy, r in each_row():
        pos[k, 16 + r : 20 + r, :] = pos_copy[k, cp, cy]
        vel[k, r : r + 4, :] = vel_copy[k, cp, cy]
    pl.semaphore_wait(barrier, len(peers))
    used = [0]

    def post(source, target, where):
        n = used[0]
        used[0] = n + 1
        copy = pltpu.make_async_remote_copy(
            src_ref=source,
            dst_ref=target,
            send_sem=send.at[n],
            recv_sem=recv.at[n],
            device_id=where,
            device_id_type=MESH,
        )
        copy.start()
        return copy

    flying = [
        post(listing, tab_land.at[0], east),
        post(listing, tab_land.at[1], west),
        post(pos.at[:, pl.ds(32, 16), :], pos_land.at[0], east),
        post(pos.at[:, pl.ds(16, 16), :], pos_land.at[1], west),
    ]
    for copy in flying:
        copy.wait()
    lane = lax.broadcasted_iota(jnp.int32, (16, 128), 1)
    joined = jnp.where(lane < 16, pltpu.roll(tab_land[0], 112, 1), pltpu.roll(listing[...], 16, 1))
    table[...] = jnp.where(lane < 48, joined, pltpu.roll(tab_land[1], 48, 1))
    fetch = pltpu.make_async_copy(table, tab, local.at[0])
    fetch.start()
    pos[:, 0:16, :] = pos_land[0]
    pos[:, 48:64, :] = pos_land[1]
    fetch.wait()

    lane = lax.broadcasted_iota(jnp.int32, (1, 128), 1)

    def mask_row(c, carry):
        live = lane < tab[0, c + 16]
        occ[pl.ds(c, 1), :] = jnp.where(live, KICK_SCALE, 0.0)
        for k in range(3):
            vel[k, pl.ds(c, 1), :] = jnp.where(live, vel[k, pl.ds(c, 1), :], 0.0)
        return carry

    lax.fori_loop(0, 32, mask_row, 0, unroll=8)
    relays = []
    for step in range(QUENCH):
        last = step == QUENCH - 1
        prepare_positions(pos, tab, left, spread, pick)
        density_pass(pos, tab, emb, left, off, own)
        flying = [
            post(emb.at[pl.ds(32, 16), :], emb_land.at[step, 0], east),
            post(emb.at[pl.ds(16, 16), :], emb_land.at[step, 1], west),
        ]
        if last:
            for copy in relays:
                copy.wait()
            relay[...] = shared[...] + rep_land[0] + rep_land[1] + rep_land[2]
            relays = [post(relay, rep_land.at[n], (across(rep, REP_HOPS[n]), me)) for n in (3, 4, 5)]
        prepare_embed(16, 32, emb, left)
        for copy in flying:
            copy.wait()
        emb[0:16, :] = emb_land[step, 0]
        emb[48:64, :] = emb_land[step, 1]
        prepare_embed(0, 16, emb, left)
        prepare_embed(48, 16, emb, left)
        force_pass(pos, tab, emb, frc, left, spread, off, own)
        vel[...] = vel[...] + STEP_SIZE * frc[...]
        motion, forces = vel[...], frc[...]
        part[step] = jnp.concatenate([squares(motion), squares(forces), jnp.zeros((6, 128), F32)], axis=0)
        flying = [post(part.at[step], slots.at[step, n], (rep, p)) for n, p in enumerate(places)]
        if not last:
            for n, source in enumerate((vel, frc)):
                flying.append(post(source.at[:, pl.ds(16, 16), :], vf_land.at[0, n], east))
                flying.append(post(source.at[:, pl.ds(0, 16), :], vf_land.at[1, n], west))
            mine = jnp.where(rep == exit_in[0], 1.0, 0.0)
            shared[0:3] = pos[:, 16:48, :] * mine
            shared[3:6] = motion * mine
            relays = [post(shared, rep_land.at[n], (across(rep, REP_HOPS[n]), me)) for n in (0, 1, 2)]
        else:
            for copy in relays:
                copy.wait()
            for n in range(6):
                shared[n] = relay[n] + rep_land[3, n] + rep_land[4, n] + rep_land[5, n]
            for k, cp, cy, r in each_row():
                pos_out[0, k, cp, cy] = pos[k, 16 + r : 20 + r, :]
                vel_out[0, k, cp, cy] = vel[k, r : r + 4, :]
                frc_out[0, k, cp, cy] = frc[k, r : r + 4, :]
                xpos_out[0, k, cp, cy] = shared[k, r : r + 4, :]
                xvel_out[0, k, cp, cy] = shared[3 + k, r : r + 4, :]
                if k == 0:
                    occ_out[cp, cy] = occ[r : r + 4, :]
        for copy in flying:
            copy.wait()
        total = part[step]
        for n in range(size - 1):
            total = total + slots[step, n]
        total = jnp.sum(total, axis=1, keepdims=True)
        mixing = ALPHA_MIX * jnp.sqrt(total[0:1] / (total[1:2] + EPSILON))
        if last:
            mix_out[...] = jnp.broadcast_to(mixing, (1, 128))
        else:
            mixing = mixing[None]
            new = (1.0 - ALPHA_MIX) * motion + mixing * forces
            vel[...] = new
            pos[:, 16:48, :] = pos[:, 16:48, :] + STEP_SIZE * new
            for n, rows in enumerate((slice(0, 16), slice(48, 64))):
                moved = (1.0 - ALPHA_MIX) * vf_land[n, 0] + mixing * vf_land[n, 1]
                pos[:, rows, :] = pos[:, rows, :] + STEP_SIZE * moved


def body(positions, velocities, thermal_noise, counts, pair_flags, exit_replica):
    size = lax.axis_size("space")
    table = jnp.pad(pair_flags.transpose(1, 2, 3, 0), ((0, 0),) * 3 + ((1, 114),))
    first = lax.broadcasted_iota(jnp.int32, table.shape, 3) == 0
    table = jnp.where(first, counts[..., None], table)
    vm = pl.BlockSpec(memory_space=pltpu.VMEM)
    sm = pl.BlockSpec(memory_space=pltpu.SMEM)
    copies = 4 + QUENCH * (2 + size - 1) + 4 + len(REP_HOPS)
    pos, vel, frc, xpos, xvel, kick, mixing = pl.pallas_call(
        functools.partial(whole_kernel, size),
        out_shape=(jax.ShapeDtypeStruct(positions.shape, F32),) * 5 + (
            jax.ShapeDtypeStruct((2, 4, 4, 128), F32),
            jax.ShapeDtypeStruct((1, 128), F32),
        ),
        in_specs=[pl.BlockSpec(memory_space=pltpu.HBM)] * 2 + [vm, sm],
        out_specs=(vm,) * 7,
        scratch_shapes=[
            pltpu.VMEM((3, 64, 128), F32),
            pltpu.VMEM((3, 32, 128), F32),
            pltpu.VMEM((3, 32, 128), F32),
            pltpu.VMEM((64, 128), F32),
            pltpu.VMEM((64, 128, DEPTH), BF16),
            pltpu.VMEM((64, 3, 128, 128), F32),
            pltpu.VMEM((3, 32, 128), F32),
            pltpu.VMEM((4, 6, 32, 128), F32),
            pltpu.VMEM((DEPTH, 384), BF16),
            pltpu.VMEM((2, 3, 16, 128), F32),
            pltpu.VMEM((2, 16, 128), jnp.int32),
            pltpu.VMEM((QUENCH, 2, 16, 128), F32),
            pltpu.VMEM((2, 2, 3, 16, 128), F32),
            pltpu.VMEM((QUENCH, 8, 128), F32),
            pltpu.VMEM((QUENCH, size - 1, 8, 128), F32),
            pltpu.VMEM((6, 32, 128), F32),
            pltpu.VMEM((6, 32, 128), F32),
            pltpu.VMEM((len(REP_HOPS), 6, 32, 128), F32),
            pltpu.VMEM((3, 2, 4, 4, 128), F32),
            pltpu.VMEM((3, 2, 4, 4, 128), F32),
            pltpu.VMEM((32, 128), F32),
            pltpu.VMEM((16, 128), jnp.int32),
            pltpu.VMEM((16, 128), jnp.int32),
            pltpu.SMEM((16, 128), jnp.int32),
            pltpu.SemaphoreType.DMA((copies,)),
            pltpu.SemaphoreType.DMA((copies,)),
            pltpu.SemaphoreType.DMA((3,)),
        ],
        compiler_params=pltpu.CompilerParams(
            collective_id=1, has_side_effects=True, vmem_limit_bytes=58 << 20
        ),
    )(positions, velocities, table, exit_replica)
    quench_vel = (1.0 - ALPHA_MIX) * vel + mixing.reshape(128) * frc
    dephase_vel = FRICTION * xvel + kick * thermal_noise[0]
    return pos + STEP_SIZE * quench_vel, quench_vel, xpos + STEP_SIZE * dephase_vel, dephase_vel


def solution(mesh):
    atoms = P("rep", None, "space", None, None, None)
    placed = (
        atoms,
        atoms,
        P("rep", None, None, "space", None, None, None),
        P("space", None, None),
        P(None, "space", None, None),
        P(),
    )
    return jax.shard_map(body, mesh=mesh, in_specs=placed, out_specs=(atoms,) * 4, check_vma=False)
```
